128 devices in a mesh: wide: 16 (over z_lo, x, core), narrow: 8 (over y, z_hi).
Axes of the slice: x: 4, y: 4, z: 4 (z_hi: 2, z_lo: 2; z = z_hi * 2 + z_lo), core: 2. Of those that a mesh axis runs over, the one named last changes fastest.
Arguments:
- x_stash: bfloat16 [1536, 8192], P('wide', 'narrow'), may hold values from -6 to 6
- token_ids: int32 [1024], P('wide'), may hold values from 0 to 1535, as said below
- grad_out: bfloat16 [1024, 8192], P('wide', 'narrow'), may hold values from -1.5 to 1.5
- w_up: bfloat16 [8192, 30720], P('narrow', 'wide'), may hold values from -0.0625 to 0.0625
- w_down: bfloat16 [8192, 30720], P('narrow', 'wide'), may hold values from -0.03125 to 0.03125
- acc_up: bfloat16 [8, 16, 1966592], P('narrow', 'wide'), may hold values from -6 to 6
- acc_down: bfloat16 [8, 16, 1966592], P('narrow', 'wide'), may hold values from -6 to 6
- offsets: int32 [2, 8, 16], P(None, 'narrow', 'wide'), may hold values from 0 to 512, as said below
Outputs:
- out_y: bfloat16 [1024, 8192], P('wide', 'narrow')
- grad_in: bfloat16 [1024, 8192], P('wide', 'narrow')
- new_up: bfloat16 [8192, 30720], P('narrow', 'wide')
- new_down: bfloat16 [8192, 30720], P('narrow', 'wide')
The draws below stay inside these ranges and needn't reach their ends.
Inputs may be any that keep to these rules, and one draw needn't show every extreme that they name: `token_ids`: entries j * 64 to (j + 1) * 64 - 1 are distinct rows between j * 96 and (j + 1) * 96 - 1. `offsets`: multiples of 128.
All inputs are finite; a program needn't handle non-finite values.
Results may differ from the reference program's by a relative error of at most 0.005.
Values may be sent and summed in bfloat16 or wider, within the bound.
No kernel may reach another device: no remote copies, remote signals or barrier semaphores. Data moves between devices by JAX's collectives and lax.ppermute only.
A program may use at most 192 MiB of HBM per device.

```python
import jax
import jax.numpy as jnp
from jax import lax

D = 8192
F = 30720
TOK_DEV = 64
STASH_DEV = 96
SLACK = 512
ZN = 8
ZW = 16
TOK = 1024
STASH = 1536
SHARD = 1966080
BUF = 1966592


def draw_token_ids(key, part):
    key = jax.random.fold_in(key, 11)
    blocks = TOK // TOK_DEV
    block_keys = jax.random.split(key, blocks)
    orders = jax.vmap(lambda one_key: jax.random.permutation(one_key, STASH_DEV))(block_keys)
    shifts = jax.random.randint(jax.random.fold_in(key, 5), (blocks,), 0, STASH_DEV)
    shifts = shifts.at[0].set(0).at[blocks - 1].set(STASH_DEV - 1)
    chosen = orders[:, :TOK_DEV]
    places = (chosen - chosen[:, :1] + shifts[:, None]) % STASH_DEV
    places = places + jnp.arange(blocks, dtype=jnp.int32)[:, None] * STASH_DEV
    return places.reshape(TOK).astype(jnp.int32)


def draw_offsets(key, part):
    key = jax.random.fold_in(key, 23)
    starts = jax.random.randint(key, (2, ZN, ZW), 0, SLACK // 128 + 1) * 128
    starts = starts.at[0, 0, 0].set(SLACK).at[1, ZN - 1, ZW - 1].set(0)
    return starts.astype(jnp.int32)


def shard_levels(rng, dims, cuts, smallest, high):
    factor_of = 1.0
    for position, shards_of in cuts:
        heights = jax.random.uniform(jax.random.fold_in(jax.random.fold_in(rng, 6), position), (shards_of,), jnp.float32, smallest / len(cuts), high / len(cuts))
        factor_of = factor_of * jnp.repeat(jnp.exp(heights), dims[position] // shards_of).reshape((-1,) + (1,) * (len(dims) - 1 - position))
    return factor_of


def noise(key, extent, width, limit, shards=(), held_as=jnp.bfloat16):
    gain = shard_levels(key, extent, shards, -0.22, 0.18) if shards else 1.0
    drawn = jax.random.normal(key, extent, jnp.float32) * width * gain
    return jnp.minimum(jnp.maximum(drawn, -limit), limit).astype(held_as)


def setup_inputs(seed: int = 0) -> dict:
    seeds = jax.random.split(jax.random.key(seed), 9)
    return {
        "x_stash": noise(seeds[0], (STASH, D), 1.0, 6.0, ((0, 16), (1, 8))),
        "token_ids": draw_token_ids(jax.random.fold_in(seeds[8], 71), 0),
        "grad_out": noise(seeds[2], (TOK, D), 0.25, 1.5, ((0, 16), (1, 8))),
        "w_up": noise(seeds[3], (D, F), D ** -0.5, 0.0625, ((0, 8), (1, 16))),
        "w_down": noise(seeds[4], (D, F), F ** -0.5, 0.03125, ((0, 8), (1, 16))),
        "acc_up": noise(seeds[5], (ZN, ZW, BUF), 1.0, 6.0, ((0, 8), (1, 16))),
        "acc_down": noise(seeds[6], (ZN, ZW, BUF), 1.0, 6.0, ((0, 8), (1, 16))),
        "offsets": draw_offsets(jax.random.fold_in(seeds[8], 71), 0),
    }


def gelu_parts(hidden):
    normal_cdf = 0.5 * (1.0 + jax.scipy.special.erf(hidden * 0.7071067811865476))
    density = jnp.exp(-0.5 * hidden * hidden) * 0.3989422804014327
    return hidden * normal_cdf, normal_cdf + hidden * density


def take_segment(buffer, start):
    return lax.dynamic_slice_in_dim(buffer, start.astype(jnp.int32), SHARD)


def to_blocks(accum, starts):
    segments = jax.vmap(jax.vmap(take_segment))(accum, starts)
    return segments.reshape(D, F)


def reference(x_stash, token_ids, grad_out, w_up, w_down, acc_up, acc_down, offsets):
    inputs = x_stash[token_ids]
    hidden = jnp.dot(inputs, w_up, preferred_element_type=jnp.float32)
    gelu_value, slope = gelu_parts(hidden)
    activation = gelu_value.astype(jnp.bfloat16)
    out_y = jnp.dot(activation, w_down.T, preferred_element_type=jnp.float32).astype(jnp.bfloat16)
    back = jnp.dot(grad_out, w_down, preferred_element_type=jnp.float32)
    hidden_grad = (back * slope).astype(jnp.bfloat16)
    grad_in = jnp.dot(hidden_grad, w_up.T, preferred_element_type=jnp.float32).astype(jnp.bfloat16)
    up_blocks = to_blocks(acc_up, offsets[0])
    new_up = (up_blocks.astype(jnp.float32) + jnp.dot(inputs.T, hidden_grad, preferred_element_type=jnp.float32)).astype(jnp.bfloat16)
    down_blocks = to_blocks(acc_down, offsets[1])
    new_down = (down_blocks.astype(jnp.float32) + jnp.dot(grad_out.T, activation, preferred_element_type=jnp.float32)).astype(jnp.bfloat16)
    return (out_y, grad_in, new_up, new_down)
```

```python
import functools

import jax
import jax.numpy as jnp
from jax import lax
from jax.experimental import pallas as pl
from jax.experimental.pallas import tpu as pltpu
from jax.sharding import PartitionSpec as P

SLACK = 512
MIB = 2**20
BF16 = jnp.bfloat16
F32 = jnp.float32
WIDE = "wide"
NARROW = "narrow"

CORE_SWAP = [(k, k ^ 1) for k in range(16)]
Z_SWAP = [(k, k ^ 8) for k in range(16)]
X_SHIFT = [[(k, (k & 8) | ((k + 2 * d) & 7)) for k in range(16)] for d in range(4)]
ZHI_SWAP = [(k, k ^ 1) for k in range(8)]
Y_RIGHT = [(k, (k + 2) % 8) for k in range(8)]
Y_LEFT = [(k, (k - 2) % 8) for k in range(8)]
PLANES = [list(range(8)), list(range(8, 16))]
CB = 384
DB = 256


def sds(shape, dtype):
    return jax.ShapeDtypeStruct(shape, dtype)


def cost(flops, nbytes):
    return pl.CostEstimate(flops=int(flops), bytes_accessed=int(nbytes), transcendentals=0)


def gelu_parts(hidden):
    normal_cdf = 0.5 * (1.0 + jax.scipy.special.erf(hidden * 0.7071067811865476))
    density = jnp.exp(-0.5 * hidden * hidden) * 0.3989422804014327
    return (hidden * normal_cdf, normal_cdf + hidden * density)


HBM = pl.BlockSpec(memory_space=pl.ANY)


def call(kernel, place, grid, ins, outs, scratch, mib, work, name, after=()):
    n, m = len(ins), len(after)

    def run(s_ref, *refs):
        kernel(s_ref, *refs[:n], *refs[n + m :])

    return pl.pallas_call(
        run,
        out_shape=[shape for shape, _, _ in outs],
        grid_spec=pltpu.PrefetchScalarGridSpec(
            num_scalar_prefetch=1,
            grid=grid,
            in_specs=[pl.BlockSpec(block, index) for _, block, index in ins] + [HBM] * m,
            out_specs=[pl.BlockSpec(block, index) for _, block, index in outs],
            scratch_shapes=scratch,
        ),
        compiler_params=pltpu.CompilerParams(vmem_limit_bytes=mib * MIB),
        cost_estimate=cost(*work),
        name=name,
    )(place, *[a for a, _, _ in ins], *after)


def whole(a):
    zeros = (0,) * a.ndim
    return (a, a.shape, lambda i, s: zeros)


def col(a):
    return (a, (a.shape[0], CB), lambda j, s: (0, j))


def pick_kernel(s_ref, ids_ref, stash_ref, grad_ref, out_ref, wide, rows):
    tokens = grad_ref.shape[0]
    n = tokens // 4
    wide[...] = stash_ref[...].astype(F32)
    for d in range(4):
        group = (s_ref[0] + d) % 4
        at = tokens + d * n
        out_ref[at : at + n] = grad_ref[pl.ds(pl.multiple_of(group * n, n), n)]
        for i in range(n):
            row = ids_ref[group * n + i] - s_ref[5]
            rows[d * n + i : d * n + i + 1] = wide[pl.ds(row, 1)]
    out_ref[:tokens] = rows[...].astype(BF16)


def simple_call(kernel, ins, outs, scratch, nbytes, name, after=(), mib=16):
    n, m = len(ins), len(after)

    def run(*refs):
        kernel(*refs[:n], *refs[n + m :])

    def spec(a):
        return pl.BlockSpec(memory_space=pltpu.SMEM if a.dtype == jnp.int32 else pltpu.VMEM)

    return pl.pallas_call(
        run,
        out_shape=outs,
        in_specs=[spec(a) for a in ins] + [HBM] * m,
        out_specs=[pl.BlockSpec(memory_space=pltpu.VMEM)] * len(outs),
        scratch_shapes=scratch,
        compiler_params=pltpu.CompilerParams(vmem_limit_bytes=mib * MIB),
        cost_estimate=cost(0, nbytes),
        name=name,
    )(*ins, *after)


def pick(place, ids, stash, grad):
    return simple_call(
        pick_kernel,
        [place, ids, stash, grad],
        [sds((2 * grad.shape[0], grad.shape[1]), BF16)],
        [pltpu.VMEM(stash.shape, F32), pltpu.VMEM(grad.shape, F32)],
        2e6,
        "pick",
    )[0]


def hold(x, after):
    return pl.pallas_call(
        lambda *refs: None,
        out_shape=sds(x.shape, x.dtype),
        in_specs=[HBM] * (1 + len(after)),
        out_specs=HBM,
        input_output_aliases={0: 0},
        cost_estimate=cost(0, 0),
        name="hold",
    )(x, *after)


def join_kernel(*refs):
    at = 0
    for ref in refs[:-1]:
        refs[-1][at : at + ref.shape[0]] = ref[...]
        at += ref.shape[0]


def join(blocks, name, after=()):
    rows = sum(b.shape[0] for b in blocks)
    return simple_call(join_kernel, blocks, [sds((rows, *blocks[0].shape[1:]), BF16)], [], 2e6, name, after)[0]


STEP = 16


def relay_kernel(s_ref, up_ref, down_ref, own_ref, over_ref, seg, rows, sem):
    parts, _, width = rows.shape
    plane = parts // 2
    line = parts * width
    chunks = own_ref.shape[2] // STEP
    z = s_ref[2]
    for i, ref in enumerate((up_ref, down_ref)):
        for c in range(chunks):
            at = pl.multiple_of(s_ref[3 + i] + c * STEP * line, 128)
            k = i * chunks + c
            pltpu.make_async_copy(ref.at[:, :, pl.ds(at, STEP * line)], seg.at[k], sem.at[k]).start()
    for i, ref in enumerate((up_ref, down_ref)):
        for c in range(chunks):
            k = i * chunks + c
            pltpu.make_async_copy(ref.at[:, :, pl.ds(0, STEP * line)], seg.at[k], sem.at[k]).wait()

            @pl.loop(0, STEP)
            def _(r):
                for w in range(parts):
                    at = pl.multiple_of(r * line + w * width, 128)
                    rows[w, pl.ds(r, 1), :] = seg[k, 0, :, pl.ds(at, width)].astype(F32)

            @pl.loop(0, plane)
            def _(w):
                own_ref[w, i, c * STEP : (c + 1) * STEP] = rows[z * plane + w].astype(BF16)
                over_ref[w, i, c * STEP : (c + 1) * STEP] = rows[(1 - z) * plane + w].astype(BF16)


def relay(place, acc_up, acc_down, width, parts, after=()):
    line = width * parts
    n_rows = (acc_up.shape[2] - SLACK) // line
    plane = parts // 2
    n = len(after)

    def run(s_ref, up_ref, down_ref, *refs):
        relay_kernel(s_ref, up_ref, down_ref, *refs[n:])

    return pl.pallas_call(
        run,
        out_shape=[sds((plane, 2, n_rows, width), BF16)] * 2,
        in_specs=[pl.BlockSpec(memory_space=pltpu.SMEM)] + [HBM] * (2 + n),
        out_specs=[pl.BlockSpec(memory_space=pltpu.VMEM)] * 2,
        scratch_shapes=[
            pltpu.VMEM((2 * n_rows // STEP, 1, 1, STEP * line), BF16),
            pltpu.VMEM((parts, STEP, width), F32),
            pltpu.SemaphoreType.DMA((2 * n_rows // STEP,)),
        ],
        compiler_params=pltpu.CompilerParams(vmem_limit_bytes=32 * MIB),
        cost_estimate=cost(0, 32e6),
        name="relay",
    )(place, acc_up, acc_down, *after)


def rows_of(ref0, ref1):
    depth = ref0.shape[-1]
    return jnp.concatenate([ref0[...].reshape(-1, depth), ref1[...].reshape(-1, depth)], axis=0)


def far_kernel(s_ref, x0_ref, x1_ref, g0_ref, g1_ref, up_ref, down_ref, a_ref, b_ref):
    half = a_ref.shape[1]
    for i, (r0, r1, w_ref) in enumerate(((x0_ref, x1_ref, up_ref), (g0_ref, g1_ref, down_ref))):
        total = jnp.dot(rows_of(r0, r1), w_ref[...], preferred_element_type=F32)
        a_ref[i] = total[:half].astype(BF16)
        b_ref[i] = total[half:].astype(BF16)


def near_kernel(s_ref, r0_ref, r1_ref, l0_ref, l1_ref, w_ref, a_ref, b_ref, right_ref, left_ref):
    half = a_ref.shape[1]
    right = jnp.dot(rows_of(r0_ref, r1_ref), w_ref[...], preferred_element_type=F32)
    right_ref[:half] = (right[:half] + a_ref[0].astype(F32)).astype(BF16)
    right_ref[half:] = right[half:].astype(BF16)
    left = jnp.dot(rows_of(l0_ref, l1_ref), w_ref[...], preferred_element_type=F32)
    left_ref[:half] = left[:half].astype(BF16)
    left_ref[half:] = (left[half:] + b_ref[0].astype(F32)).astype(BF16)


def own_kernel(s_ref, x0_ref, x1_ref, w_ref, p1_ref, p3_ref, keep_ref, send_ref):
    half = keep_ref.shape[0]
    total = jnp.dot(rows_of(x0_ref, x1_ref), w_ref[...], preferred_element_type=F32)
    total = total + p1_ref[...].astype(F32) + p3_ref[...].astype(F32)
    first = s_ref[1] == 0
    keep_ref[...] = jnp.where(first, total[:half], total[half:])
    send_ref[...] = jnp.where(first, total[half:], total[:half]).astype(BF16)


def rows_spec(a, i, k):
    blocks, _, _, r, depth = a.shape
    return (a, (blocks, None, 1, r, depth), lambda j, s: (0, i, k, 0, 0))


def layer(a, i):
    return (a, (1, a.shape[1], CB), lambda j, s: (i, 0, j))


def half_rows(x):
    return x[0].shape[0] * x[0].shape[3]


def feature_call(kernel, place, rows, ws, extra, outs, name, after=()):
    depth, width = ws[0].shape
    m = 128 * len(rows)
    return call(
        kernel,
        place,
        (width // CB,),
        rows + [col(w) for w in ws] + extra,
        outs,
        [],
        20,
        (2 * m * depth * width, 2 * depth * width + 2 * m * width),
        name,
        after,
    )


def far_sum(place, x, w_up, w_down, after=()):
    width = w_up.shape[1]
    out = layer(sds((2, half_rows(x), width), BF16), 0)
    out = (out[0], (2, half_rows(x), CB), lambda j, s: (0, 0, j))
    rows = [rows_spec(a, i, 2) for i in range(2) for a in x]
    a, b = feature_call(far_kernel, place, rows, (w_up, w_down), [], [out, out], "far", after)
    return (lax.ppermute(a, NARROW, Y_RIGHT), lax.ppermute(b, NARROW, Y_LEFT)), a


def near_sum(place, x, i, w, terms, tag, after=()):
    out = col(sds((2 * half_rows(x), w.shape[1]), BF16))
    rows = [rows_spec(a, i, k) for k in (1, 3) for a in x]
    extra = [layer(t, i) for t in terms]
    right, left = feature_call(near_kernel, place, rows, (w,), extra, [out, out], tag + "_near", after)
    return (lax.ppermute(right, NARROW, Y_RIGHT), lax.ppermute(left, NARROW, Y_LEFT)), right


def own_sum(place, x, i, w, terms, tag, after=()):
    outs = [col(sds((half_rows(x), w.shape[1]), dtype)) for dtype in (F32, BF16)]
    rows = [rows_spec(a, i, 0) for a in x]
    keep, send = feature_call(own_kernel, place, rows, (w,), [col(t) for t in terms], outs, tag + "_own", after)
    return keep, lax.ppermute(send, NARROW, ZHI_SWAP), send


def narrow_gather(mine, other, tag, after):
    half = mine.shape[0]
    own = join([mine, other], "join_" + tag, after)
    prev, nxt = lax.ppermute(own, NARROW, Y_RIGHT), lax.ppermute(own, NARROW, Y_LEFT)
    far_m, far_o = lax.ppermute(prev[:half], NARROW, Y_RIGHT), lax.ppermute(nxt[half:], NARROW, Y_LEFT)
    return [own, nxt, prev], [far_m, far_o]


def rows_kernel(s_ref, *refs):
    pieces, w_ref, out0_ref, out1_ref, held = refs[:-4], refs[-4], refs[-3], refs[-2], refs[-1]
    groups, _, half, width = held.shape

    @pl.when(pl.program_id(0) == 0)
    def _():
        at = 0
        for ref in pieces:
            for i in range(ref.shape[0] // half):
                second = s_ref[1] if at % 2 == 0 else 1 - s_ref[1]
                held[at // 2, second] = ref[i * half : (i + 1) * half]
                at += 1

    total = lax.dot_general(
        held[...].reshape(-1, width), w_ref[...], (((1,), (1,)), ((), ())), preferred_element_type=F32
    )
    for g in range(groups):
        at = g * 2 * half
        out0_ref[g] = total[at : at + half]
        out1_ref[g] = total[at + half : at + 2 * half]


def rows_call(place, pieces, half, w, name, after=()):
    width = pieces[0].shape[1]
    depth = w.shape[0]
    groups = sum(a.shape[0] for a in pieces) // (2 * half)

    def out():
        return (sds((groups, half, depth), F32), (groups, half, DB), lambda j, s: (0, 0, j))

    return call(
        rows_kernel,
        place,
        (depth // DB,),
        [whole(a) for a in pieces] + [(w, (DB, width), lambda j, s: (j, 0))],
        [out(), out()],
        [pltpu.VMEM((groups, 2, half, width), BF16)],
        30,
        (4 * groups * half * depth * width, 2 * depth * width + 4 * groups * half * (width + 4 * depth)),
        name,
        after,
    )


def merge_kernel(*refs):
    own_ref, outs = refs[-4], refs[-3:]
    n = (len(refs) - 4) // 2
    b = own_ref.shape[1]
    at = 0
    for i in range(n):
        for g in range(refs[i].shape[0]):
            own_ref[at] = refs[i][g, :b] + refs[n + i][g, :b]
            for d in range(1, 4):
                rows = slice(d * b, (d + 1) * b)
                outs[d - 1][at] = (refs[i][g, rows] + refs[n + i][g, rows]).astype(BF16)
            at += 1


def cross_kernel(own_ref, *refs):
    keep_ref, send_ref = refs[-2:]
    r = keep_ref.shape[1]
    for g in range(own_ref.shape[0]):
        total = own_ref[g] + refs[0][g].astype(F32) + refs[1][g].astype(F32) + refs[2][g].astype(F32)
        keep_ref[g] = total[:r]
        send_ref[g] = total[r:].astype(BF16)


def finish_kernel(s_ref, keep_ref, other_ref, out_ref):
    r = keep_ref.shape[1]
    for i, d in enumerate((0, 1, 3, 2)):
        at = pl.multiple_of(((s_ref[0] + d) % 4) * r, r)
        out_ref[pl.ds(at, r)] = (keep_ref[i] + other_ref[i].astype(F32)).astype(BF16)


def wide_sum(place, kept, given, tag, later):
    taken = lax.ppermute(given, WIDE, CORE_SWAP)
    groups, rows, depth = kept.shape
    b, r = rows // 4, rows // 8
    outs = [sds((groups, b, depth), F32)] + [sds((groups, b, depth), BF16)] * 3
    own, *blocks = simple_call(merge_kernel, [kept, taken], outs, [], 8e6, "merge_" + tag, (), 20)
    got = [lax.ppermute(block, WIDE, X_SHIFT[d]) for d, block in zip((1, 2, 3), blocks)]
    outs = [sds((groups, r, depth), F32), sds((groups, r, depth), BF16)]
    keep, send = simple_call(cross_kernel, [own, *got], outs, [], 2e6, "cross_" + tag, later(own))
    other = lax.ppermute(send, WIDE, Z_SWAP)
    outs = [sds((groups * r, depth), BF16)]
    return simple_call(finish_kernel, [place, keep, other], outs, [], 1e6, "finish_" + tag)[0], own, send


def wide_gather(rows, work):
    pair = jnp.stack([rows, lax.ppermute(rows, WIDE, Z_SWAP)])
    after = work(pair)
    blocks = [pair] + [lax.ppermute(pair, WIDE, X_SHIFT[(4 - d) % 4]) for d in (1, 2, 3)]
    mine = join(blocks, "join_rows", after)
    theirs = lax.ppermute(mine, WIDE, CORE_SWAP)
    shape = (mine.shape[0], 2, 4, mine.shape[1] // 8, mine.shape[2])
    return [mine.reshape(shape), theirs.reshape(shape)], after


def update_kernel(s_ref, x0_ref, x1_ref, *refs):
    pieces, own_ref, other_ref, out_ref, turned = refs[:5], refs[5], refs[6], refs[7], refs[8]
    half, cols = pieces[4].shape
    depth = out_ref.shape[0]

    @pl.when(pl.program_id(0) == 0)
    def _():
        for i, g in enumerate((0, 1, 3, 2)):
            for core, ref in enumerate((x0_ref, x1_ref)):
                second = s_ref[1] if core == 0 else 1 - s_ref[1]
                at = pl.multiple_of((2 * i + second) * half, 128)
                turned[:, pl.ds(at, half)] = ref[:, g].reshape(half, depth).T

    rhs = jnp.concatenate([p[...] for p in pieces], axis=0)
    first = s_ref[2] == 0
    own = own_ref[...].reshape(depth // 2, cols)
    other = other_ref[...].reshape(depth // 2, cols)
    for i in range(2):
        at = i * (depth // 2)
        total = jnp.dot(turned[at : at + depth // 2], rhs, preferred_element_type=F32)
        block = jnp.where(first, own, other) if i == 0 else jnp.where(first, other, own)
        out_ref[at : at + depth // 2] = (total + block.astype(F32)).astype(BF16)


def update_call(place, x, k, pieces, own, which, other, name, after=()):
    half, width = pieces[4].shape
    blocks, _, groups, r, depth = x[0].shape
    plane, _, n_rows, _ = other.shape
    return call(
        update_kernel,
        place,
        (width // CB,),
        [(a, (blocks, None, groups, r, depth), lambda j, s: (0, k, 0, 0, 0)) for a in x]
        + [col(a) for a in pieces]
        + [
            (own, (plane, 1, n_rows, CB), lambda j, s: (0, which, 0, j)),
            (other, (plane, 1, n_rows, CB), lambda j, s: (0, which, 0, j)),
        ],
        [col(sds((depth, width), BF16))],
        [pltpu.VMEM((depth, 8 * half), BF16)],
        32,
        (16 * half * depth * width, 16 * half * (depth + width) + 4 * depth * width),
        name,
        after,
    )[0]


def body(x_stash, token_ids, grad_out, w_up, w_down, acc_up, acc_down, offsets):
    narrow, wide = lax.axis_index(NARROW), lax.axis_index(WIDE)
    parts = lax.axis_size(WIDE)
    width = w_up.shape[1]
    where = jnp.stack([narrow // 2, narrow % 2, wide // 8]).astype(jnp.int32)
    base = (wide * x_stash.shape[0]).astype(jnp.int32)
    place = jnp.concatenate([where, offsets.reshape(2), base[None]])

    x, (own, over) = wide_gather(
        pick(place, token_ids, x_stash, grad_out),
        lambda pair: relay(place, acc_up, acc_down, width, parts, (pair,)),
    )
    half = half_rows(x)

    far, far_done = far_sum(place, x, w_up, w_down, ())
    near_h, done = near_sum(place, x, 0, w_up, far, "hidden", (far_done,))
    near_b, done = near_sum(place, x, 1, w_down, far, "back", (done,))
    over = lax.ppermute(hold(over, (far_done,)), WIDE, Z_SWAP)
    own_blocks = lax.all_to_all(hold(own, (far_done,)), WIDE, 0, 0, tiled=True, axis_index_groups=PLANES)
    keep, other, done = own_sum(place, x, 0, w_up, near_h, "hidden", (done,))
    gelu_value, slope = gelu_parts(keep + other.astype(F32))
    mine = gelu_value.astype(BF16)
    act_other = lax.ppermute(mine, NARROW, ZHI_SWAP)
    keep, other, done = own_sum(place, x, 1, w_down, near_b, "back", (act_other,))
    held = hold(over, (done,))
    other_blocks = lax.all_to_all(held, WIDE, 0, 0, tiled=True, axis_index_groups=PLANES)
    act, act_far = narrow_gather(mine, act_other, "act", (done, own_blocks))
    hidden_grad = ((keep + other.astype(F32)) * slope).astype(BF16)
    grad, grad_far = narrow_gather(hidden_grad, lax.ppermute(hidden_grad, NARROW, ZHI_SWAP), "grad", (act_far[0], act_far[1]))
    k0, g0 = rows_call(place, act + act_far, half, w_down, "out_rows", (grad[0],))
    k1, g1 = rows_call(place, grad + grad_far, half, w_up, "grad_rows", (g0, other_blocks))
    results = {}

    def grad_first(own_out):
        results["grad"] = wide_sum(place, k1, g1, "grad", lambda own: ())
        return (results["grad"][1],)

    out_y, _, out_sent = wide_sum(place, k0, g0, "out", grad_first)
    grad_in, own, sent = results["grad"]
    after = (own, out_sent)
    new_up = update_call(place, x, 0, grad + grad_far, own_blocks, 0, other_blocks, "up_update", after)
    new_down = update_call(place, x, 1, act + act_far, own_blocks, 1, other_blocks, "down_update", (new_up, sent))
    return (out_y, grad_in, new_up, new_down)


def solution(mesh):
    in_specs = (
        P("wide", "narrow"),
        P("wide"),
        P("wide", "narrow"),
        P("narrow", "wide"),
        P("narrow", "wide"),
        P("narrow", "wide", None),
        P("narrow", "wide", None),
        P(None, "narrow", "wide"),
    )
    out_specs = (P("wide", "narrow"), P("wide", "narrow"), P("narrow", "wide"), P("narrow", "wide"))
    return jax.shard_map(body, mesh=mesh, in_specs=in_specs, out_specs=out_specs, check_vma=False)
```

```python
import functools

import jax
import jax.numpy as jnp
from jax import lax
from jax.experimental import pallas as pl
from jax.experimental.pallas import tpu as pltpu
from jax.sharding import PartitionSpec as P

SLACK = 512
MIB = 2**20
BF16 = jnp.bfloat16
F32 = jnp.float32
WIDE = "wide"
NARROW = "narrow"

CORE_SWAP = [(k, k ^ 1) for k in range(16)]
Z_SWAP = [(k, k ^ 8) for k in range(16)]
X_SHIFT = [[(k, (k & 8) | ((k + 2 * d) & 7)) for k in range(16)] for d in range(4)]
ZHI_SWAP = [(k, k ^ 1) for k in range(8)]
Y_RIGHT = [(k, (k + 2) % 8) for k in range(8)]
Y_LEFT = [(k, (k - 2) % 8) for k in range(8)]
CB = 384
DB = 256


def sds(shape, dtype):
    return jax.ShapeDtypeStruct(shape, dtype)


def cost(flops, nbytes):
    return pl.CostEstimate(flops=int(flops), bytes_accessed=int(nbytes), transcendentals=0)


def gelu_parts(hidden):
    normal_cdf = 0.5 * (1.0 + jax.scipy.special.erf(hidden * 0.7071067811865476))
    density = jnp.exp(-0.5 * hidden * hidden) * 0.3989422804014327
    return (hidden * normal_cdf, normal_cdf + hidden * density)


HBM = pl.BlockSpec(memory_space=pl.ANY)


def call(kernel, place, grid, ins, outs, scratch, mib, work, name, after=()):
    n, m = len(ins), len(after)

    def spec(block, index):
        return pl.BlockSpec(memory_space=pltpu.HBM) if block is None else pl.BlockSpec(block, index)

    def run(s_ref, *refs):
        kernel(s_ref, *refs[:n], *refs[n + m :])

    return pl.pallas_call(
        run,
        out_shape=[shape for shape, _, _ in outs],
        grid_spec=pltpu.PrefetchScalarGridSpec(
            num_scalar_prefetch=1,
            grid=grid,
            in_specs=[spec(block, index) for _, block, index in ins] + [HBM] * m,
            out_specs=[pl.BlockSpec(block, index) for _, block, index in outs],
            scratch_shapes=scratch,
        ),
        compiler_params=pltpu.CompilerParams(vmem_limit_bytes=mib * MIB),
        cost_estimate=cost(*work),
        name=name,
    )(place, *[a for a, _, _ in ins], *after)


def whole(a):
    zeros = (0,) * a.ndim
    return (a, a.shape, lambda i, s: zeros)


def col(a):
    return (a, (a.shape[0], CB), lambda j, s: (0, j))


def pick_kernel(s_ref, ids_ref, stash_ref, grad_ref, out_ref, wide, rows):
    tokens = grad_ref.shape[0]
    n = tokens // 4
    wide[...] = stash_ref[...].astype(F32)
    for d in range(4):
        group = (s_ref[0] + d) % 4
        at = tokens + d * n
        out_ref[at : at + n] = grad_ref[pl.ds(pl.multiple_of(group * n, n), n)]
        for i in range(n):
            row = ids_ref[group * n + i] - s_ref[5]
            rows[d * n + i : d * n + i + 1] = wide[pl.ds(row, 1)]
    out_ref[:tokens] = rows[...].astype(BF16)


def simple_call(kernel, ins, outs, scratch, nbytes, name, after=(), mib=50):
    n, m = len(ins), len(after)

    def run(*refs):
        kernel(*refs[:n], *refs[n + m :])

    def spec(a):
        return pl.BlockSpec(memory_space=pltpu.SMEM if a.dtype == jnp.int32 else pltpu.VMEM)

    return pl.pallas_call(
        run,
        out_shape=outs,
        in_specs=[spec(a) for a in ins] + [HBM] * m,
        out_specs=[pl.BlockSpec(memory_space=pltpu.VMEM)] * len(outs),
        scratch_shapes=scratch,
        compiler_params=pltpu.CompilerParams(vmem_limit_bytes=mib * MIB),
        cost_estimate=cost(0, nbytes),
        name=name,
    )(*ins, *after)


def pick(place, ids, stash, grad):
    return simple_call(
        pick_kernel,
        [place, ids, stash, grad],
        [sds((2 * grad.shape[0], grad.shape[1]), BF16)],
        [pltpu.VMEM(stash.shape, F32), pltpu.VMEM(grad.shape, F32)],
        2e6,
        "pick",
    )[0]


def hold(x, after):
    return pl.pallas_call(
        lambda *refs: None,
        out_shape=sds(x.shape, x.dtype),
        in_specs=[HBM] * (1 + len(after)),
        out_specs=HBM,
        input_output_aliases={0: 0},
        cost_estimate=cost(0, 0),
        name="hold",
    )(x, *after)


def join_kernel(*refs):
    at = 0
    for ref in refs[:-1]:
        refs[-1][at : at + ref.shape[0]] = ref[...]
        at += ref.shape[0]


def join(blocks, name, after=()):
    rows = sum(b.shape[0] for b in blocks)
    return simple_call(join_kernel, blocks, [sds((rows, *blocks[0].shape[1:]), BF16)], [], 2e6, name, after)[0]


STEP = 16


def relay_kernel(s_ref, up_ref, down_ref, to_up_ref, to_down_ref, seg, rows, sem):
    parts, _, width = rows.shape
    line = parts * width
    chunks = to_up_ref.shape[1] // STEP
    for i, ref in enumerate((up_ref, down_ref)):
        for c in range(chunks):
            at = pl.multiple_of(s_ref[3 + i] + c * STEP * line, 128)
            k = i * chunks + c
            pltpu.make_async_copy(ref.at[:, :, pl.ds(at, STEP * line)], seg.at[k], sem.at[k]).start()
    for i, ref in enumerate((up_ref, down_ref)):
        out_ref = (to_up_ref, to_down_ref)[i]
        for c in range(chunks):
            k = i * chunks + c
            pltpu.make_async_copy(ref.at[:, :, pl.ds(0, STEP * line)], seg.at[k], sem.at[k]).wait()

            @pl.loop(0, STEP)
            def _(r):
                for w in range(parts):
                    at = pl.multiple_of(r * line + w * width, 128)
                    rows[w, pl.ds(r, 1), :] = seg[k, 0, :, pl.ds(at, width)].astype(F32)

            @pl.loop(0, parts)
            def _(w):
                out_ref[w, c * STEP : (c + 1) * STEP] = rows[w].astype(BF16)


def relay(place, acc_up, acc_down, width, parts, after=()):
    line = width * parts
    n_rows = (acc_up.shape[2] - SLACK) // line
    n = len(after)

    def run(s_ref, up_ref, down_ref, *refs):
        relay_kernel(s_ref, up_ref, down_ref, *refs[n:])

    return pl.pallas_call(
        run,
        out_shape=[sds((parts, n_rows, width), BF16)] * 2,
        in_specs=[pl.BlockSpec(memory_space=pltpu.SMEM)] + [HBM] * (2 + n),
        out_specs=[pl.BlockSpec(memory_space=pltpu.VMEM)] * 2,
        scratch_shapes=[
            pltpu.VMEM((2 * n_rows // STEP, 1, 1, STEP * line), BF16),
            pltpu.VMEM((parts, STEP, width), F32),
            pltpu.SemaphoreType.DMA((2 * n_rows // STEP,)),
        ],
        compiler_params=pltpu.CompilerParams(vmem_limit_bytes=32 * MIB),
        cost_estimate=cost(0, 32e6),
        name="relay",
    )(place, acc_up, acc_down, *after)


def rows_of(ref0, ref1):
    depth = ref0.shape[-1]
    return jnp.concatenate([ref0[...].reshape(-1, depth), ref1[...].reshape(-1, depth)], axis=0)


def far_kernel(s_ref, x0_ref, x1_ref, g0_ref, g1_ref, up_ref, down_ref, a_ref, b_ref):
    half = a_ref.shape[1]
    for i, (r0, r1, w_ref) in enumerate(((x0_ref, x1_ref, up_ref), (g0_ref, g1_ref, down_ref))):
        total = jnp.dot(rows_of(r0, r1), w_ref[...], preferred_element_type=F32)
        a_ref[i] = total[:half].astype(BF16)
        b_ref[i] = total[half:].astype(BF16)


def near_kernel(s_ref, r0_ref, r1_ref, l0_ref, l1_ref, w_ref, a_ref, b_ref, right_ref, left_ref):
    half = a_ref.shape[1]
    right = jnp.dot(rows_of(r0_ref, r1_ref), w_ref[...], preferred_element_type=F32)
    right_ref[:half] = (right[:half] + a_ref[0].astype(F32)).astype(BF16)
    right_ref[half:] = right[half:].astype(BF16)
    left = jnp.dot(rows_of(l0_ref, l1_ref), w_ref[...], preferred_element_type=F32)
    left_ref[:half] = left[:half].astype(BF16)
    left_ref[half:] = (left[half:] + b_ref[0].astype(F32)).astype(BF16)


def own_kernel(s_ref, x0_ref, x1_ref, w_ref, p1_ref, p3_ref, keep_ref, send_ref):
    half = keep_ref.shape[0]
    total = jnp.dot(rows_of(x0_ref, x1_ref), w_ref[...], preferred_element_type=F32)
    total = total + p1_ref[...].astype(F32) + p3_ref[...].astype(F32)
    first = s_ref[1] == 0
    keep_ref[...] = jnp.where(first, total[:half], total[half:])
    send_ref[...] = jnp.where(first, total[half:], total[:half]).astype(BF16)


def rows_spec(a, i, k):
    blocks, _, _, r, depth = a.shape
    return (a, (blocks, None, 1, r, depth), lambda j, s: (0, i, k, 0, 0))


def layer(a, i):
    return (a, (1, a.shape[1], CB), lambda j, s: (i, 0, j))


def half_rows(x):
    return x[0].shape[0] * x[0].shape[3]


def feature_call(kernel, place, rows, ws, extra, outs, name, after=()):
    depth, width = ws[0].shape
    m = 128 * len(rows)
    return call(
        kernel,
        place,
        (width // CB,),
        rows + [col(w) for w in ws] + extra,
        outs,
        [],
        20,
        (2 * m * depth * width, 2 * depth * width + 2 * m * width),
        name,
        after,
    )


def far_sum(place, x, w_up, w_down, after=()):
    width = w_up.shape[1]
    out = layer(sds((2, half_rows(x), width), BF16), 0)
    out = (out[0], (2, half_rows(x), CB), lambda j, s: (0, 0, j))
    rows = [rows_spec(a, i, 2) for i in range(2) for a in x]
    a, b = feature_call(far_kernel, place, rows, (w_up, w_down), [], [out, out], "far", after)
    return (lax.ppermute(a, NARROW, Y_RIGHT), lax.ppermute(b, NARROW, Y_LEFT)), a


def near_sum(place, x, i, w, terms, tag, after=()):
    out = col(sds((2 * half_rows(x), w.shape[1]), BF16))
    rows = [rows_spec(a, i, k) for k in (1, 3) for a in x]
    extra = [layer(t, i) for t in terms]
    right, left = feature_call(near_kernel, place, rows, (w,), extra, [out, out], tag + "_near", after)
    return (lax.ppermute(right, NARROW, Y_RIGHT), lax.ppermute(left, NARROW, Y_LEFT)), right


def own_sum(place, x, i, w, terms, tag, after=()):
    outs = [col(sds((half_rows(x), w.shape[1]), dtype)) for dtype in (F32, BF16)]
    rows = [rows_spec(a, i, 0) for a in x]
    keep, send = feature_call(own_kernel, place, rows, (w,), [col(t) for t in terms], outs, tag + "_own", after)
    return keep, lax.ppermute(send, NARROW, ZHI_SWAP), send


def far_gather(pieces, after):
    _, nxt, prev = pieces
    half = nxt.shape[0] // 2
    near = prev[:half], nxt[half:]
    if after:
        near = [hold(a, after) for a in near]
    return [lax.ppermute(near[0], NARROW, Y_RIGHT), lax.ppermute(near[1], NARROW, Y_LEFT)]


def narrow_gather(mine, other, tag, after, far=True):
    own = join([mine, other], "join_" + tag, after)
    prev, nxt = lax.ppermute(own, NARROW, Y_RIGHT), lax.ppermute(own, NARROW, Y_LEFT)
    pieces = [own, nxt, prev]
    return pieces, far_gather(pieces, ()) if far else None


def exchange(blocks):
    return lax.all_to_all(blocks, WIDE, 0, 0, tiled=True)


def rows_kernel(s_ref, *refs):
    pieces, (w_ref, out0_ref, out1_ref, held, sem) = refs[:-5], refs[-5:]
    _, _, half, width = held.shape

    @pl.when(pl.program_id(0) == 0)
    def _():
        copies = []
        for ref in pieces:
            for i in range(ref.shape[0] // half):
                at = len(copies)
                second = s_ref[1] if at % 2 == 0 else 1 - s_ref[1]
                copy = pltpu.make_async_copy(ref.at[pl.ds(i * half, half)], held.at[at // 2, second], sem.at[at])
                copy.start()
                copies.append(copy)
        for copy in copies:
            copy.wait()

    total = lax.dot_general(
        held[...].reshape(-1, width), w_ref[...], (((1,), (1,)), ((), ())), preferred_element_type=F32
    )
    for g in range(held.shape[0]):
        at = g * 2 * half
        out0_ref[g] = total[at : at + half]
        out1_ref[g] = total[at + half : at + 2 * half]


def rows_call(place, pieces, half, w, name, after=()):
    width = pieces[0].shape[1]
    depth = w.shape[0]
    groups = sum(a.shape[0] for a in pieces) // (2 * half)

    def out():
        return (sds((groups, half, depth), F32), (groups, half, DB), lambda j, s: (0, 0, j))

    return call(
        rows_kernel,
        place,
        (depth // DB,),
        [(a, None, None) for a in pieces] + [(w, (DB, width), lambda j, s: (j, 0))],
        [out(), out()],
        [pltpu.VMEM((groups, 2, half, width), BF16), pltpu.SemaphoreType.DMA((2 * groups,))],
        50,
        (4 * groups * half * depth * width, 2 * depth * width + 4 * groups * half * (width + 4 * depth)),
        name,
        after,
    )


def merge_kernel(*refs):
    own_ref, outs = refs[-4], refs[-3:]
    n = (len(refs) - 4) // 2
    b = own_ref.shape[1]
    at = 0
    for i in range(n):
        for g in range(refs[i].shape[0]):
            own_ref[at] = refs[i][g, :b] + refs[n + i][g, :b]
            for d in range(1, 4):
                rows = slice(d * b, (d + 1) * b)
                outs[d - 1][at] = (refs[i][g, rows] + refs[n + i][g, rows]).astype(BF16)
            at += 1


def cross_kernel(own_ref, *refs):
    keep_ref, send_ref = refs[-2:]
    r = keep_ref.shape[1]
    for g in range(own_ref.shape[0]):
        total = own_ref[g] + refs[0][g].astype(F32) + refs[1][g].astype(F32) + refs[2][g].astype(F32)
        keep_ref[g] = total[:r]
        send_ref[g] = total[r:].astype(BF16)


def finish_kernel(s_ref, keep_ref, other_ref, out_ref):
    r = keep_ref.shape[1]
    for i, d in enumerate((0, 1, 3, 2)):
        at = pl.multiple_of(((s_ref[0] + d) % 4) * r, r)
        out_ref[pl.ds(at, r)] = (keep_ref[i] + other_ref[i].astype(F32)).astype(BF16)


def wide_sum(place, kept, given, tag, later):
    taken = lax.ppermute(given, WIDE, CORE_SWAP)
    groups, rows, depth = kept.shape
    b, r = rows // 4, rows // 8
    outs = [sds((groups, b, depth), F32)] + [sds((groups, b, depth), BF16)] * 3
    own, *blocks = simple_call(merge_kernel, [kept, taken], outs, [], 8e6, "merge_" + tag)
    got = [lax.ppermute(block, WIDE, X_SHIFT[d]) for d, block in zip((1, 2, 3), blocks)]
    outs = [sds((groups, r, depth), F32), sds((groups, r, depth), BF16)]
    keep, send = simple_call(cross_kernel, [own, *got], outs, [], 2e6, "cross_" + tag, later(own))
    other = lax.ppermute(send, WIDE, Z_SWAP)
    outs = [sds((groups * r, depth), BF16)]
    return simple_call(finish_kernel, [place, keep, other], outs, [], 1e6, "finish_" + tag)[0], own, send


def wide_gather(rows, work):
    pair = jnp.stack([rows, lax.ppermute(rows, WIDE, Z_SWAP)])
    after = work(pair)
    blocks = [pair] + [lax.ppermute(pair, WIDE, X_SHIFT[(4 - d) % 4]) for d in (1, 2, 3)]
    mine = join(blocks, "join_rows")
    theirs = lax.ppermute(mine, WIDE, CORE_SWAP)
    shape = (mine.shape[0], 2, 4, mine.shape[1] // 8, mine.shape[2])
    return [mine.reshape(shape), theirs.reshape(shape)], after, mine


def update_kernel(s_ref, x0_ref, x1_ref, *refs):
    pieces, blocks_ref, out_ref, turned = refs[:5], refs[5], refs[6], refs[7]
    half, cols = pieces[4].shape
    depth = out_ref.shape[0]

    @pl.when(pl.program_id(0) == 0)
    def _():
        for i, g in enumerate((0, 1, 3, 2)):
            for core, ref in enumerate((x0_ref, x1_ref)):
                second = s_ref[1] if core == 0 else 1 - s_ref[1]
                at = pl.multiple_of((2 * i + second) * half, 128)
                turned[:, pl.ds(at, half)] = ref[:, g].reshape(half, depth).T

    rhs = jnp.concatenate([p[...] for p in pieces], axis=0)
    total = jnp.dot(turned[...], rhs, preferred_element_type=F32)
    out_ref[...] = (total + blocks_ref[...].reshape(depth, cols).astype(F32)).astype(BF16)


def update_call(place, x, k, pieces, gathered, name, after=()):
    half, width = pieces[4].shape
    blocks, _, groups, r, depth = x[0].shape
    parts, n_rows, _ = gathered.shape
    return call(
        update_kernel,
        place,
        (width // CB,),
        [(a, (blocks, None, groups, r, depth), lambda j, s: (0, k, 0, 0, 0)) for a in x]
        + [col(a) for a in pieces]
        + [(gathered, (parts, n_rows, CB), lambda j, s: (0, 0, j))],
        [col(sds((depth, width), BF16))],
        [pltpu.VMEM((depth, 8 * half), BF16)],
        50,
        (16 * half * depth * width, 16 * half * (depth + width) + 4 * depth * width),
        name,
        after,
    )[0]


def body(x_stash, token_ids, grad_out, w_up, w_down, acc_up, acc_down, offsets):
    narrow, wide = lax.axis_index(NARROW), lax.axis_index(WIDE)
    parts = lax.axis_size(WIDE)
    width = w_up.shape[1]
    where = jnp.stack([narrow // 2, narrow % 2, wide // 8]).astype(jnp.int32)
    base = (wide * x_stash.shape[0]).astype(jnp.int32)
    place = jnp.concatenate([where, offsets.reshape(2), base[None]])

    x, (to_up, to_down), joined = wide_gather(
        pick(place, token_ids, x_stash, grad_out),
        lambda pair: relay(place, acc_up, acc_down, width, parts, (pair,)),
    )
    half = half_rows(x)

    far, far_done = far_sum(place, x, w_up, w_down, ())
    up_blocks = exchange(hold(to_up, (joined,)))
    near_h, done = near_sum(place, x, 0, w_up, far, "hidden", (far_done,))
    near_b, done = near_sum(place, x, 1, w_down, far, "back", (done,))

    keep, other, done = own_sum(place, x, 0, w_up, near_h, "hidden", (done,))
    gelu_value, slope = gelu_parts(keep + other.astype(F32))
    mine = gelu_value.astype(BF16)
    act_other = lax.ppermute(mine, NARROW, ZHI_SWAP)
    keep, other, done = own_sum(place, x, 1, w_down, near_b, "back", (act_other, up_blocks))
    act, act_far = narrow_gather(mine, act_other, "act", (done,))
    hidden_grad = ((keep + other.astype(F32)) * slope).astype(BF16)
    grad_other = lax.ppermute(hidden_grad, NARROW, ZHI_SWAP)
    to_down = hold(to_down, (grad_other,))
    down_blocks = exchange(to_down)
    grad, _ = narrow_gather(hidden_grad, grad_other, "grad", (act_far[0], act_far[1], to_down), False)
    kept, given = rows_call(place, act + act_far, half, w_down, "out_rows", (grad[0],))
    near_done = (grad[1], grad[2])
    grad_far = far_gather(grad, (given, *near_done))
    given = hold(given, near_done)
    results = {}

    def grad_first(own_out):
        results["rows"] = rows_call(place, grad + grad_far, half, w_up, "grad_rows", (own_out,))
        return (results["rows"][1], down_blocks)

    out_y, _, out_sent = wide_sum(place, kept, given, "out", grad_first)
    kept, given = results["rows"]

    def up_first(own):
        results["up"] = update_call(place, x, 0, grad + grad_far, up_blocks, "up_update", (own,))
        return (results["up"],)

    grad_in, _, sent = wide_sum(place, kept, hold(given, (out_sent,)), "grad", up_first)
    new_up = results["up"]
    new_down = update_call(place, x, 1, act + act_far, down_blocks, "down_update", (sent,))
    return (out_y, grad_in, new_up, new_down)


def solution(mesh):
    in_specs = (
        P("wide", "narrow"),
        P("wide"),
        P("wide", "narrow"),
        P("narrow", "wide"),
        P("narrow", "wide"),
        P("narrow", "wide", None),
        P("narrow", "wide", None),
        P(None, "narrow", "wide"),
    )
    out_specs = (P("wide", "narrow"), P("wide", "narrow"), P("narrow", "wide"), P("narrow", "wide"))
    return jax.shard_map(body, mesh=mesh, in_specs=in_specs, out_specs=out_specs, check_vma=False)
```

```python
import functools

import jax
import jax.numpy as jnp
from jax import lax
from jax.experimental import pallas as pl
from jax.experimental.pallas import tpu as pltpu
from jax.sharding import PartitionSpec as P

SLACK = 512
MIB = 2**20
SMALL = 16
WIDE_GRANT = 62
BF16 = jnp.bfloat16
F32 = jnp.float32
WIDE = "wide"
NARROW = "narrow"

CORE_SWAP = [(k, k ^ 1) for k in range(16)]
Z_SWAP = [(k, k ^ 8) for k in range(16)]
X_SHIFT = [[(k, (k & 8) | ((k + 2 * d) & 7)) for k in range(16)] for d in range(4)]
ZHI_SWAP = [(k, k ^ 1) for k in range(8)]
Y_RIGHT = [(k, (k + 2) % 8) for k in range(8)]
Y_LEFT = [(k, (k - 2) % 8) for k in range(8)]
CB = 384
DB = 256


def sds(shape, dtype):
    return jax.ShapeDtypeStruct(shape, dtype)


def cost(flops, nbytes):
    return pl.CostEstimate(flops=int(flops), bytes_accessed=int(nbytes), transcendentals=0)


def gelu_parts(hidden):
    normal_cdf = 0.5 * (1.0 + jax.scipy.special.erf(hidden * 0.7071067811865476))
    density = jnp.exp(-0.5 * hidden * hidden) * 0.3989422804014327
    return (hidden * normal_cdf, normal_cdf + hidden * density)


HBM = pl.BlockSpec(memory_space=pl.ANY)


def call(kernel, place, grid, ins, outs, scratch, mib, work, name, after=()):
    n, m = len(ins), len(after)

    def spec(block, index):
        return pl.BlockSpec(memory_space=pltpu.HBM) if block is None else pl.BlockSpec(block, index)

    def run(s_ref, *refs):
        kernel(s_ref, *refs[:n], *refs[n + m :])

    return pl.pallas_call(
        run,
        out_shape=[shape for shape, _, _ in outs],
        grid_spec=pltpu.PrefetchScalarGridSpec(
            num_scalar_prefetch=1,
            grid=grid,
            in_specs=[spec(block, index) for _, block, index in ins] + [HBM] * m,
            out_specs=[pl.BlockSpec(block, index) for _, block, index in outs],
            scratch_shapes=scratch,
        ),
        compiler_params=pltpu.CompilerParams(vmem_limit_bytes=mib * MIB),
        cost_estimate=cost(*work),
        name=name,
    )(place, *[a for a, _, _ in ins], *after)


def whole(a):
    zeros = (0,) * a.ndim
    return (a, a.shape, lambda i, s: zeros)


def col(a):
    return (a, (a.shape[0], CB), lambda j, s: (0, j))


def pick_kernel(s_ref, ids_ref, stash_ref, grad_ref, out_ref, wide, rows):
    tokens = grad_ref.shape[0]
    n = tokens // 4
    wide[...] = stash_ref[...].astype(F32)
    for d in range(4):
        group = (s_ref[0] + d) % 4
        at = tokens + d * n
        out_ref[at : at + n] = grad_ref[pl.ds(pl.multiple_of(group * n, n), n)]
        for i in range(n):
            row = ids_ref[group * n + i] - s_ref[5]
            rows[d * n + i : d * n + i + 1] = wide[pl.ds(row, 1)]
    out_ref[:tokens] = rows[...].astype(BF16)


def simple_call(kernel, ins, outs, scratch, nbytes, name, after=(), mib=SMALL):
    n, m = len(ins), len(after)

    def run(*refs):
        kernel(*refs[:n], *refs[n + m :])

    def spec(a):
        return pl.BlockSpec(memory_space=pltpu.SMEM if a.dtype == jnp.int32 else pltpu.VMEM)

    return pl.pallas_call(
        run,
        out_shape=outs,
        in_specs=[spec(a) for a in ins] + [HBM] * m,
        out_specs=[pl.BlockSpec(memory_space=pltpu.VMEM)] * len(outs),
        scratch_shapes=scratch,
        compiler_params=pltpu.CompilerParams(vmem_limit_bytes=mib * MIB),
        cost_estimate=cost(0, nbytes),
        name=name,
    )(*ins, *after)


def pick(place, ids, stash, grad):
    return simple_call(
        pick_kernel,
        [place, ids, stash, grad],
        [sds((2 * grad.shape[0], grad.shape[1]), BF16)],
        [pltpu.VMEM(stash.shape, F32), pltpu.VMEM(grad.shape, F32)],
        2e6,
        "pick",
    )[0]


def hold(x, after):
    return pl.pallas_call(
        lambda *refs: None,
        out_shape=sds(x.shape, x.dtype),
        in_specs=[HBM] * (1 + len(after)),
        out_specs=HBM,
        input_output_aliases={0: 0},
        cost_estimate=cost(0, 0),
        name="hold",
    )(x, *after)


def join_kernel(*refs):
    at = 0
    for ref in refs[:-1]:
        refs[-1][at : at + ref.shape[0]] = ref[...]
        at += ref.shape[0]


def join(blocks, name, after=()):
    rows = sum(b.shape[0] for b in blocks)
    return simple_call(join_kernel, blocks, [sds((rows, *blocks[0].shape[1:]), BF16)], [], 2e6, name, after)[0]


STEP = 16


def relay_kernel(s_ref, up_ref, down_ref, to_up_ref, to_down_ref, seg, rows, sem):
    parts, _, width = rows.shape
    line = parts * width
    chunks = to_up_ref.shape[1] // STEP
    for i, ref in enumerate((up_ref, down_ref)):
        for c in range(chunks):
            at = pl.multiple_of(s_ref[3 + i] + c * STEP * line, 128)
            k = i * chunks + c
            pltpu.make_async_copy(ref.at[:, :, pl.ds(at, STEP * line)], seg.at[k], sem.at[k]).start()
    for i, ref in enumerate((up_ref, down_ref)):
        out_ref = (to_up_ref, to_down_ref)[i]
        for c in range(chunks):
            k = i * chunks + c
            pltpu.make_async_copy(ref.at[:, :, pl.ds(0, STEP * line)], seg.at[k], sem.at[k]).wait()

            @pl.loop(0, STEP)
            def _(r):
                for w in range(parts):
                    at = pl.multiple_of(r * line + w * width, 128)
                    rows[w, pl.ds(r, 1), :] = seg[k, 0, :, pl.ds(at, width)].astype(F32)

            @pl.loop(0, parts)
            def _(w):
                out_ref[w, c * STEP : (c + 1) * STEP] = rows[w].astype(BF16)


def relay(place, acc_up, acc_down, width, parts, after=()):
    line = width * parts
    n_rows = (acc_up.shape[2] - SLACK) // line
    n = len(after)

    def run(s_ref, up_ref, down_ref, *refs):
        relay_kernel(s_ref, up_ref, down_ref, *refs[n:])

    return pl.pallas_call(
        run,
        out_shape=[sds((parts, n_rows, width), BF16)] * 2,
        in_specs=[pl.BlockSpec(memory_space=pltpu.SMEM)] + [HBM] * (2 + n),
        out_specs=[pl.BlockSpec(memory_space=pltpu.VMEM)] * 2,
        scratch_shapes=[
            pltpu.VMEM((2 * n_rows // STEP, 1, 1, STEP * line), BF16),
            pltpu.VMEM((parts, STEP, width), F32),
            pltpu.SemaphoreType.DMA((2 * n_rows // STEP,)),
        ],
        compiler_params=pltpu.CompilerParams(vmem_limit_bytes=32 * MIB),
        cost_estimate=cost(0, 32e6),
        name="relay",
    )(place, acc_up, acc_down, *after)


def rows_of(ref0, ref1):
    depth = ref0.shape[-1]
    return jnp.concatenate([ref0[...].reshape(-1, depth), ref1[...].reshape(-1, depth)], axis=0)


def far_kernel(s_ref, x0_ref, x1_ref, g0_ref, g1_ref, up_ref, down_ref, a_ref, b_ref):
    half = a_ref.shape[1]
    for i, (r0, r1, w_ref) in enumerate(((x0_ref, x1_ref, up_ref), (g0_ref, g1_ref, down_ref))):
        total = jnp.dot(rows_of(r0, r1), w_ref[...], preferred_element_type=F32)
        a_ref[i] = total[:half].astype(BF16)
        b_ref[i] = total[half:].astype(BF16)


def near_kernel(s_ref, r0_ref, r1_ref, l0_ref, l1_ref, w_ref, a_ref, b_ref, right_ref, left_ref):
    half = a_ref.shape[1]
    right = jnp.dot(rows_of(r0_ref, r1_ref), w_ref[...], preferred_element_type=F32)
    right_ref[:half] = (right[:half] + a_ref[0].astype(F32)).astype(BF16)
    right_ref[half:] = right[half:].astype(BF16)
    left = jnp.dot(rows_of(l0_ref, l1_ref), w_ref[...], preferred_element_type=F32)
    left_ref[:half] = left[:half].astype(BF16)
    left_ref[half:] = (left[half:] + b_ref[0].astype(F32)).astype(BF16)


def own_kernel(s_ref, x0_ref, x1_ref, w_ref, p1_ref, p3_ref, keep_ref, send_ref):
    half = keep_ref.shape[0]
    total = jnp.dot(rows_of(x0_ref, x1_ref), w_ref[...], preferred_element_type=F32)
    total = total + p1_ref[...].astype(F32) + p3_ref[...].astype(F32)
    first = s_ref[1] == 0
    keep_ref[...] = jnp.where(first, total[:half], total[half:])
    send_ref[...] = jnp.where(first, total[half:], total[:half]).astype(BF16)


def rows_spec(a, i, k):
    blocks, _, _, r, depth = a.shape
    return (a, (blocks, None, 1, r, depth), lambda j, s: (0, i, k, 0, 0))


def layer(a, i):
    return (a, (1, a.shape[1], CB), lambda j, s: (i, 0, j))


def half_rows(x):
    return x[0].shape[0] * x[0].shape[3]


def feature_call(kernel, place, rows, ws, extra, outs, name, after=()):
    depth, width = ws[0].shape
    m = 128 * len(rows)
    return call(
        kernel,
        place,
        (width // CB,),
        rows + [col(w) for w in ws] + extra,
        outs,
        [],
        20,
        (2 * m * depth * width, 2 * depth * width + 2 * m * width),
        name,
        after,
    )


def far_sum(place, x, w_up, w_down, after=()):
    width = w_up.shape[1]
    out = layer(sds((2, half_rows(x), width), BF16), 0)
    out = (out[0], (2, half_rows(x), CB), lambda j, s: (0, 0, j))
    rows = [rows_spec(a, i, 2) for i in range(2) for a in x]
    a, b = feature_call(far_kernel, place, rows, (w_up, w_down), [], [out, out], "far", after)
    return (lax.ppermute(a, NARROW, Y_RIGHT), lax.ppermute(b, NARROW, Y_LEFT)), a


def near_sum(place, x, i, w, terms, tag, after=()):
    out = col(sds((2 * half_rows(x), w.shape[1]), BF16))
    rows = [rows_spec(a, i, k) for k in (1, 3) for a in x]
    extra = [layer(t, i) for t in terms]
    right, left = feature_call(near_kernel, place, rows, (w,), extra, [out, out], tag + "_near", after)
    return (lax.ppermute(right, NARROW, Y_RIGHT), lax.ppermute(left, NARROW, Y_LEFT)), right


def own_sum(place, x, i, w, terms, tag, after=()):
    outs = [col(sds((half_rows(x), w.shape[1]), dtype)) for dtype in (F32, BF16)]
    rows = [rows_spec(a, i, 0) for a in x]
    keep, send = feature_call(own_kernel, place, rows, (w,), [col(t) for t in terms], outs, tag + "_own", after)
    return keep, lax.ppermute(send, NARROW, ZHI_SWAP), send


def far_gather(pieces, after):
    _, nxt, prev = pieces
    half = nxt.shape[0] // 2
    near = prev[:half], nxt[half:]
    if after:
        near = [hold(a, after) for a in near]
    return [lax.ppermute(near[0], NARROW, Y_RIGHT), lax.ppermute(near[1], NARROW, Y_LEFT)]


def narrow_gather(mine, other, tag, after, far=True):
    own = join([mine, other], "join_" + tag, after)
    prev, nxt = lax.ppermute(own, NARROW, Y_RIGHT), lax.ppermute(own, NARROW, Y_LEFT)
    pieces = [own, nxt, prev]
    return pieces, far_gather(pieces, ()) if far else None


def exchange(blocks):
    return lax.all_to_all(blocks, WIDE, 0, 0, tiled=True)


def rows_kernel(s_ref, *refs):
    pieces, (w_ref, out0_ref, out1_ref, held, sem) = refs[:-5], refs[-5:]
    _, _, half, width = held.shape

    @pl.when(pl.program_id(0) == 0)
    def _():
        copies = []
        for ref in pieces:
            for i in range(ref.shape[0] // half):
                at = len(copies)
                second = s_ref[1] if at % 2 == 0 else 1 - s_ref[1]
                copy = pltpu.make_async_copy(ref.at[pl.ds(i * half, half)], held.at[at // 2, second], sem.at[at])
                copy.start()
                copies.append(copy)
        for copy in copies:
            copy.wait()

    total = lax.dot_general(
        held[...].reshape(-1, width), w_ref[...], (((1,), (1,)), ((), ())), preferred_element_type=F32
    )
    for g in range(held.shape[0]):
        at = g * 2 * half
        out0_ref[g] = total[at : at + half]
        out1_ref[g] = total[at + half : at + 2 * half]


def rows_call(place, pieces, half, w, name, after=()):
    width = pieces[0].shape[1]
    depth = w.shape[0]
    groups = sum(a.shape[0] for a in pieces) // (2 * half)

    def out():
        return (sds((groups, half, depth), F32), (groups, half, DB), lambda j, s: (0, 0, j))

    return call(
        rows_kernel,
        place,
        (depth // DB,),
        [(a, None, None) for a in pieces] + [(w, (DB, width), lambda j, s: (j, 0))],
        [out(), out()],
        [pltpu.VMEM((groups, 2, half, width), BF16), pltpu.SemaphoreType.DMA((2 * groups,))],
        50,
        (4 * groups * half * depth * width, 2 * depth * width + 4 * groups * half * (width + 4 * depth)),
        name,
        after,
    )


def merge_kernel(*refs):
    own_ref, outs = refs[-4], refs[-3:]
    n = (len(refs) - 4) // 2
    b = own_ref.shape[1]
    at = 0
    for i in range(n):
        for g in range(refs[i].shape[0]):
            own_ref[at] = refs[i][g, :b] + refs[n + i][g, :b]
            for d in range(1, 4):
                rows = slice(d * b, (d + 1) * b)
                outs[d - 1][at] = (refs[i][g, rows] + refs[n + i][g, rows]).astype(BF16)
            at += 1


def cross_kernel(own_ref, *refs):
    keep_ref, send_ref = refs[-2:]
    r = keep_ref.shape[1]
    for g in range(own_ref.shape[0]):
        total = own_ref[g] + refs[0][g].astype(F32) + refs[1][g].astype(F32) + refs[2][g].astype(F32)
        keep_ref[g] = total[:r]
        send_ref[g] = total[r:].astype(BF16)


def finish_kernel(s_ref, keep_ref, other_ref, out_ref):
    r = keep_ref.shape[1]
    for i, d in enumerate((0, 1, 3, 2)):
        at = pl.multiple_of(((s_ref[0] + d) % 4) * r, r)
        out_ref[pl.ds(at, r)] = (keep_ref[i] + other_ref[i].astype(F32)).astype(BF16)


def core_sum(kept, given, tag, after=()):
    taken = lax.ppermute(given, WIDE, CORE_SWAP)
    groups, rows, depth = kept.shape
    b = rows // 4
    outs = [sds((groups, b, depth), F32)] + [sds((groups, b, depth), BF16)] * 3
    return simple_call(merge_kernel, [kept, taken], outs, [], 8e6, "merge_" + tag, after, WIDE_GRANT)


def x_exchange(blocks):
    return [lax.ppermute(block, WIDE, X_SHIFT[d]) for d, block in zip((1, 2, 3), blocks)]


def x_sum(own, got, tag, after=()):
    groups, b, depth = own.shape
    outs = [sds((groups, b // 2, depth), F32), sds((groups, b // 2, depth), BF16)]
    return simple_call(cross_kernel, [own, *got], outs, [], 2e6, "cross_" + tag, after, WIDE_GRANT)


def z_sum(place, keep, send, tag, after=()):
    other = lax.ppermute(send, WIDE, Z_SWAP)
    outs = [sds((keep.shape[0] * keep.shape[1], keep.shape[2]), BF16)]
    return simple_call(finish_kernel, [place, keep, other], outs, [], 1e6, "finish_" + tag, after, WIDE_GRANT)[0]


def wide_gather(rows, work):
    pair = jnp.stack([rows, lax.ppermute(rows, WIDE, Z_SWAP)])
    after = work(pair)
    blocks = [pair] + [lax.ppermute(pair, WIDE, X_SHIFT[(4 - d) % 4]) for d in (1, 2, 3)]
    mine = join(blocks, "join_rows")
    theirs = lax.ppermute(mine, WIDE, CORE_SWAP)
    shape = (mine.shape[0], 2, 4, mine.shape[1] // 8, mine.shape[2])
    return [mine.reshape(shape), theirs.reshape(shape)], after, mine


def update_kernel(s_ref, x0_ref, x1_ref, *refs):
    pieces, blocks_ref, out_ref, turned = refs[:5], refs[5], refs[6], refs[7]
    half, cols = pieces[4].shape
    depth = out_ref.shape[0]

    @pl.when(pl.program_id(0) == 0)
    def _():
        for i, g in enumerate((0, 1, 3, 2)):
            for core, ref in enumerate((x0_ref, x1_ref)):
                second = s_ref[1] if core == 0 else 1 - s_ref[1]
                at = pl.multiple_of((2 * i + second) * half, 128)
                turned[:, pl.ds(at, half)] = ref[:, g].reshape(half, depth).T

    rhs = jnp.concatenate([p[...] for p in pieces], axis=0)
    total = jnp.dot(turned[...], rhs, preferred_element_type=F32)
    out_ref[...] = (total + blocks_ref[...].reshape(depth, cols).astype(F32)).astype(BF16)


def update_call(place, x, k, pieces, gathered, name, after=()):
    half, width = pieces[4].shape
    blocks, _, groups, r, depth = x[0].shape
    parts, n_rows, _ = gathered.shape
    return call(
        update_kernel,
        place,
        (width // CB,),
        [(a, (blocks, None, groups, r, depth), lambda j, s: (0, k, 0, 0, 0)) for a in x]
        + [col(a) for a in pieces]
        + [(gathered, (parts, n_rows, CB), lambda j, s: (0, 0, j))],
        [col(sds((depth, width), BF16))],
        [pltpu.VMEM((depth, 8 * half), BF16)],
        50,
        (16 * half * depth * width, 16 * half * (depth + width) + 4 * depth * width),
        name,
        after,
    )[0]


def body(x_stash, token_ids, grad_out, w_up, w_down, acc_up, acc_down, offsets):
    narrow, wide = lax.axis_index(NARROW), lax.axis_index(WIDE)
    parts = lax.axis_size(WIDE)
    width = w_up.shape[1]
    where = jnp.stack([narrow // 2, narrow % 2, wide // 8]).astype(jnp.int32)
    base = (wide * x_stash.shape[0]).astype(jnp.int32)
    place = jnp.concatenate([where, offsets.reshape(2), base[None]])

    x, (to_up, to_down), joined = wide_gather(
        pick(place, token_ids, x_stash, grad_out),
        lambda pair: relay(place, acc_up, acc_down, width, parts, (pair,)),
    )
    half = half_rows(x)

    far, far_done = far_sum(place, x, w_up, w_down, ())
    up_blocks = exchange(hold(to_up, (joined,)))
    near_h, done = near_sum(place, x, 0, w_up, far, "hidden", (far_done,))
    near_b, done = near_sum(place, x, 1, w_down, far, "back", (done,))

    keep, other, done = own_sum(place, x, 0, w_up, near_h, "hidden", (done,))
    gelu_value, slope = gelu_parts(keep + other.astype(F32))
    mine = gelu_value.astype(BF16)
    act_other = lax.ppermute(mine, NARROW, ZHI_SWAP)
    keep, other, done = own_sum(place, x, 1, w_down, near_b, "back", (act_other, up_blocks))
    act, act_far = narrow_gather(mine, act_other, "act", (done,))
    hidden_grad = ((keep + other.astype(F32)) * slope).astype(BF16)
    grad_other = lax.ppermute(hidden_grad, NARROW, ZHI_SWAP)
    to_down = hold(to_down, (grad_other,))
    down_blocks = exchange(to_down)
    grad, _ = narrow_gather(hidden_grad, grad_other, "grad", (act_far[0], act_far[1], to_down), False)
    kept, given = rows_call(place, act + act_far, half, w_down, "out_rows", (grad[0],))
    near_done = (grad[1], grad[2])
    grad_far = far_gather(grad, (given, *near_done))
    own_out, *out_blocks = core_sum(kept, hold(given, near_done), "out")
    kept, given = rows_call(place, grad + grad_far, half, w_up, "grad_rows", (own_out,))
    out_got = x_exchange(out_blocks)
    own, *blocks = core_sum(kept, hold(given, (*out_got, down_blocks)), "grad")
    got = x_exchange(blocks)
    out_keep, out_send = x_sum(own_out, out_got, "out", (own,))
    new_up = update_call(place, x, 0, grad + grad_far, up_blocks, "up_update", (own, out_send))
    keep, send = x_sum(own, got, "grad", (new_up,))
    out_y = z_sum(place, out_keep, out_send, "out", (send,))
    new_down = update_call(place, x, 1, act + act_far, down_blocks, "down_update", (send, out_y))
    grad_in = z_sum(place, keep, send, "grad", (new_down,))
    return (out_y, grad_in, new_up, new_down)


def solution(mesh):
    in_specs = (
        P("wide", "narrow"),
        P("wide"),
        P("wide", "narrow"),
        P("narrow", "wide"),
        P("narrow", "wide"),
        P("narrow", "wide", None),
        P("narrow", "wide", None),
        P(None, "narrow", "wide"),
    )
    out_specs = (P("wide", "narrow"), P("wide", "narrow"), P("narrow", "wide"), P("narrow", "wide"))
    return jax.shard_map(body, mesh=mesh, in_specs=in_specs, out_specs=out_specs, check_vma=False)
```

```python
import functools

import jax
import jax.numpy as jnp
from jax import lax
from jax.experimental import pallas as pl
from jax.experimental.pallas import tpu as pltpu
from jax.sharding import PartitionSpec as P

SLACK = 512
MIB = 2**20
SMALL = 16
WIDE_GRANT = 62
BF16 = jnp.bfloat16
F32 = jnp.float32
WIDE = "wide"
NARROW = "narrow"

CORE_SWAP = [(k, k ^ 1) for k in range(16)]
Z_SWAP = [(k, k ^ 8) for k in range(16)]
X_SHIFT = [[(k, (k & 8) | ((k + 2 * d) & 7)) for k in range(16)] for d in range(4)]
ZHI_SWAP = [(k, k ^ 1) for k in range(8)]
Y_RIGHT = [(k, (k + 2) % 8) for k in range(8)]
Y_LEFT = [(k, (k - 2) % 8) for k in range(8)]
CB = 384
DB = 256


def sds(shape, dtype):
    return jax.ShapeDtypeStruct(shape, dtype)


def cost(flops, nbytes):
    return pl.CostEstimate(flops=int(flops), bytes_accessed=int(nbytes), transcendentals=0)


def gelu_parts(hidden):
    normal_cdf = 0.5 * (1.0 + jax.scipy.special.erf(hidden * 0.7071067811865476))
    density = jnp.exp(-0.5 * hidden * hidden) * 0.3989422804014327
    return (hidden * normal_cdf, normal_cdf + hidden * density)


HBM = pl.BlockSpec(memory_space=pl.ANY)


def call(kernel, place, grid, ins, outs, scratch, mib, work, name, after=()):
    n, m = len(ins), len(after)

    def spec(block, index):
        return pl.BlockSpec(memory_space=pltpu.HBM) if block is None else pl.BlockSpec(block, index)

    def run(s_ref, *refs):
        kernel(s_ref, *refs[:n], *refs[n + m :])

    return pl.pallas_call(
        run,
        out_shape=[shape for shape, _, _ in outs],
        grid_spec=pltpu.PrefetchScalarGridSpec(
            num_scalar_prefetch=1,
            grid=grid,
            in_specs=[spec(block, index) for _, block, index in ins] + [HBM] * m,
            out_specs=[pl.BlockSpec(block, index) for _, block, index in outs],
            scratch_shapes=scratch,
        ),
        compiler_params=pltpu.CompilerParams(vmem_limit_bytes=mib * MIB),
        cost_estimate=cost(*work),
        name=name,
    )(place, *[a for a, _, _ in ins], *after)


def whole(a):
    zeros = (0,) * a.ndim
    return (a, a.shape, lambda i, s: zeros)


def col(a):
    return (a, (a.shape[0], CB), lambda j, s: (0, j))


def pick_kernel(s_ref, ids_ref, stash_ref, grad_ref, out_ref, wide, rows):
    tokens = grad_ref.shape[0]
    n = tokens // 4
    wide[...] = stash_ref[...].astype(F32)
    for d in range(4):
        group = (s_ref[0] + d) % 4
        at = tokens + d * n
        out_ref[at : at + n] = grad_ref[pl.ds(pl.multiple_of(group * n, n), n)]
        for i in range(n):
            row = ids_ref[group * n + i] - s_ref[5]
            rows[d * n + i : d * n + i + 1] = wide[pl.ds(row, 1)]
    out_ref[:tokens] = rows[...].astype(BF16)


def simple_call(kernel, ins, outs, scratch, nbytes, name, after=(), mib=SMALL):
    n, m = len(ins), len(after)

    def run(*refs):
        kernel(*refs[:n], *refs[n + m :])

    def spec(a):
        return pl.BlockSpec(memory_space=pltpu.SMEM if a.dtype == jnp.int32 else pltpu.VMEM)

    return pl.pallas_call(
        run,
        out_shape=outs,
        in_specs=[spec(a) for a in ins] + [HBM] * m,
        out_specs=[pl.BlockSpec(memory_space=pltpu.VMEM)] * len(outs),
        scratch_shapes=scratch,
        compiler_params=pltpu.CompilerParams(vmem_limit_bytes=mib * MIB),
        cost_estimate=cost(0, nbytes),
        name=name,
    )(*ins, *after)


def pick(place, ids, stash, grad):
    return simple_call(
        pick_kernel,
        [place, ids, stash, grad],
        [sds((2 * grad.shape[0], grad.shape[1]), BF16)],
        [pltpu.VMEM(stash.shape, F32), pltpu.VMEM(grad.shape, F32)],
        2e6,
        "pick",
    )[0]


def hold(x, after):
    return pl.pallas_call(
        lambda *refs: None,
        out_shape=sds(x.shape, x.dtype),
        in_specs=[HBM] * (1 + len(after)),
        out_specs=HBM,
        input_output_aliases={0: 0},
        cost_estimate=cost(0, 0),
        name="hold",
    )(x, *after)


def join_kernel(*refs):
    at = 0
    for ref in refs[:-1]:
        refs[-1][at : at + ref.shape[0]] = ref[...]
        at += ref.shape[0]


def join(blocks, name, after=()):
    rows = sum(b.shape[0] for b in blocks)
    return simple_call(join_kernel, blocks, [sds((rows, *blocks[0].shape[1:]), BF16)], [], 2e6, name, after)[0]


STEP = 16


def relay_kernel(s_ref, up_ref, down_ref, to_up_ref, to_down_ref, seg, rows, sem):
    parts, _, width = rows.shape
    line = parts * width
    chunks = to_up_ref.shape[1] // STEP
    for i, ref in enumerate((up_ref, down_ref)):
        for c in range(chunks):
            at = pl.multiple_of(s_ref[3 + i] + c * STEP * line, 128)
            k = i * chunks + c
            pltpu.make_async_copy(ref.at[:, :, pl.ds(at, STEP * line)], seg.at[k], sem.at[k]).start()
    for i, ref in enumerate((up_ref, down_ref)):
        out_ref = (to_up_ref, to_down_ref)[i]
        for c in range(chunks):
            k = i * chunks + c
            pltpu.make_async_copy(ref.at[:, :, pl.ds(0, STEP * line)], seg.at[k], sem.at[k]).wait()

            @pl.loop(0, STEP)
            def _(r):
                for w in range(parts):
                    at = pl.multiple_of(r * line + w * width, 128)
                    rows[w, pl.ds(r, 1), :] = seg[k, 0, :, pl.ds(at, width)].astype(F32)

            @pl.loop(0, parts)
            def _(w):
                out_ref[w, c * STEP : (c + 1) * STEP] = rows[w].astype(BF16)


def relay(place, acc_up, acc_down, width, parts, after=()):
    line = width * parts
    n_rows = (acc_up.shape[2] - SLACK) // line
    n = len(after)

    def run(s_ref, up_ref, down_ref, *refs):
        relay_kernel(s_ref, up_ref, down_ref, *refs[n:])

    return pl.pallas_call(
        run,
        out_shape=[sds((parts, n_rows, width), BF16)] * 2,
        in_specs=[pl.BlockSpec(memory_space=pltpu.SMEM)] + [HBM] * (2 + n),
        out_specs=[pl.BlockSpec(memory_space=pltpu.VMEM)] * 2,
        scratch_shapes=[
            pltpu.VMEM((2 * n_rows // STEP, 1, 1, STEP * line), BF16),
            pltpu.VMEM((parts, STEP, width), F32),
            pltpu.SemaphoreType.DMA((2 * n_rows // STEP,)),
        ],
        compiler_params=pltpu.CompilerParams(vmem_limit_bytes=32 * MIB),
        cost_estimate=cost(0, 32e6),
        name="relay",
    )(place, acc_up, acc_down, *after)


def rows_of(ref0, ref1):
    depth = ref0.shape[-1]
    return jnp.concatenate([ref0[...].reshape(-1, depth), ref1[...].reshape(-1, depth)], axis=0)


def far_kernel(s_ref, x0_ref, x1_ref, g0_ref, g1_ref, up_ref, down_ref, a_ref, b_ref):
    half = a_ref.shape[1]
    for i, (r0, r1, w_ref) in enumerate(((x0_ref, x1_ref, up_ref), (g0_ref, g1_ref, down_ref))):
        total = jnp.dot(rows_of(r0, r1), w_ref[...], preferred_element_type=F32)
        a_ref[i] = total[:half].astype(BF16)
        b_ref[i] = total[half:].astype(BF16)


def near_kernel(s_ref, r0_ref, r1_ref, l0_ref, l1_ref, w_ref, a_ref, b_ref, right_ref, left_ref):
    half = a_ref.shape[1]
    right = jnp.dot(rows_of(r0_ref, r1_ref), w_ref[...], preferred_element_type=F32)
    right_ref[:half] = (right[:half] + a_ref[0].astype(F32)).astype(BF16)
    right_ref[half:] = right[half:].astype(BF16)
    left = jnp.dot(rows_of(l0_ref, l1_ref), w_ref[...], preferred_element_type=F32)
    left_ref[:half] = left[:half].astype(BF16)
    left_ref[half:] = (left[half:] + b_ref[0].astype(F32)).astype(BF16)


def own_kernel(s_ref, x0_ref, x1_ref, w_ref, p1_ref, p3_ref, keep_ref, send_ref):
    half = keep_ref.shape[0]
    total = jnp.dot(rows_of(x0_ref, x1_ref), w_ref[...], preferred_element_type=F32)
    total = total + p1_ref[...].astype(F32) + p3_ref[...].astype(F32)
    first = s_ref[1] == 0
    keep_ref[...] = jnp.where(first, total[:half], total[half:])
    send_ref[...] = jnp.where(first, total[half:], total[:half]).astype(BF16)


def rows_spec(a, i, k):
    blocks, _, _, r, depth = a.shape
    return (a, (blocks, None, 1, r, depth), lambda j, s: (0, i, k, 0, 0))


def layer(a, i):
    return (a, (1, a.shape[1], CB), lambda j, s: (i, 0, j))


def half_rows(x):
    return x[0].shape[0] * x[0].shape[3]


def feature_call(kernel, place, rows, ws, extra, outs, name, after=()):
    depth, width = ws[0].shape
    m = 128 * len(rows)
    return call(
        kernel,
        place,
        (width // CB,),
        rows + [col(w) for w in ws] + extra,
        outs,
        [],
        20,
        (2 * m * depth * width, 2 * depth * width + 2 * m * width),
        name,
        after,
    )


def far_sum(place, x, w_up, w_down, after=()):
    width = w_up.shape[1]
    out = layer(sds((2, half_rows(x), width), BF16), 0)
    out = (out[0], (2, half_rows(x), CB), lambda j, s: (0, 0, j))
    rows = [rows_spec(a, i, 2) for i in range(2) for a in x]
    a, b = feature_call(far_kernel, place, rows, (w_up, w_down), [], [out, out], "far", after)
    return (lax.ppermute(a, NARROW, Y_RIGHT), lax.ppermute(b, NARROW, Y_LEFT)), a


def near_sum(place, x, i, w, terms, tag, after=()):
    out = col(sds((2 * half_rows(x), w.shape[1]), BF16))
    rows = [rows_spec(a, i, k) for k in (1, 3) for a in x]
    extra = [layer(t, i) for t in terms]
    right, left = feature_call(near_kernel, place, rows, (w,), extra, [out, out], tag + "_near", after)
    return (lax.ppermute(right, NARROW, Y_RIGHT), lax.ppermute(left, NARROW, Y_LEFT)), right


def own_sum(place, x, i, w, terms, tag, after=()):
    outs = [col(sds((half_rows(x), w.shape[1]), dtype)) for dtype in (F32, BF16)]
    rows = [rows_spec(a, i, 0) for a in x]
    keep, send = feature_call(own_kernel, place, rows, (w,), [col(t) for t in terms], outs, tag + "_own", after)
    return keep, lax.ppermute(send, NARROW, ZHI_SWAP), send


def far_gather(pieces, after):
    _, nxt, prev = pieces
    half = nxt.shape[0] // 2
    near = prev[:half], nxt[half:]
    if after:
        near = [hold(a, after) for a in near]
    return [lax.ppermute(near[0], NARROW, Y_RIGHT), lax.ppermute(near[1], NARROW, Y_LEFT)]


def narrow_gather(mine, other, tag, after, far=True):
    own = join([mine, other], "join_" + tag, after)
    prev, nxt = lax.ppermute(own, NARROW, Y_RIGHT), lax.ppermute(own, NARROW, Y_LEFT)
    pieces = [own, nxt, prev]
    return pieces, far_gather(pieces, ()) if far else None


def exchange(blocks):
    return lax.all_to_all(blocks, WIDE, 0, 0, tiled=True)


def rows_kernel(s_ref, *refs):
    pieces, (w_ref, out0_ref, out1_ref, held, sem) = refs[:-5], refs[-5:]
    _, _, half, width = held.shape

    @pl.when(pl.program_id(0) == 0)
    def _():
        copies = []
        for ref in pieces:
            for i in range(ref.shape[0] // half):
                at = len(copies)
                second = s_ref[1] if at % 2 == 0 else 1 - s_ref[1]
                copy = pltpu.make_async_copy(ref.at[pl.ds(i * half, half)], held.at[at // 2, second], sem.at[at])
                copy.start()
                copies.append(copy)
        for copy in copies:
            copy.wait()

    total = lax.dot_general(
        held[...].reshape(-1, width), w_ref[...], (((1,), (1,)), ((), ())), preferred_element_type=F32
    )
    for g in range(held.shape[0]):
        at = g * 2 * half
        out0_ref[g] = total[at : at + half]
        out1_ref[g] = total[at + half : at + 2 * half]


def rows_call(place, pieces, half, w, name, after=()):
    width = pieces[0].shape[1]
    depth = w.shape[0]
    groups = sum(a.shape[0] for a in pieces) // (2 * half)

    def out():
        return (sds((groups, half, depth), F32), (groups, half, DB), lambda j, s: (0, 0, j))

    return call(
        rows_kernel,
        place,
        (depth // DB,),
        [(a, None, None) for a in pieces] + [(w, (DB, width), lambda j, s: (j, 0))],
        [out(), out()],
        [pltpu.VMEM((groups, 2, half, width), BF16), pltpu.SemaphoreType.DMA((2 * groups,))],
        50,
        (4 * groups * half * depth * width, 2 * depth * width + 4 * groups * half * (width + 4 * depth)),
        name,
        after,
    )


def merge_kernel(*refs):
    own_ref, outs = refs[-4], refs[-3:]
    n = (len(refs) - 4) // 2
    b = own_ref.shape[1]
    at = 0
    for i in range(n):
        for g in range(refs[i].shape[0]):
            own_ref[at] = refs[i][g, :b] + refs[n + i][g, :b]
            for d in range(1, 4):
                rows = slice(d * b, (d + 1) * b)
                outs[d - 1][at] = (refs[i][g, rows] + refs[n + i][g, rows]).astype(BF16)
            at += 1


def cross_kernel(own_ref, *refs):
    keep_ref, send_ref = refs[-2:]
    r = keep_ref.shape[1]
    for g in range(own_ref.shape[0]):
        total = own_ref[g] + refs[0][g].astype(F32) + refs[1][g].astype(F32) + refs[2][g].astype(F32)
        keep_ref[g] = total[:r]
        send_ref[g] = total[r:].astype(BF16)


def finish_kernel(s_ref, keep_ref, other_ref, out_ref):
    r = keep_ref.shape[1]
    for i, d in enumerate((0, 1, 3, 2)):
        at = pl.multiple_of(((s_ref[0] + d) % 4) * r, r)
        out_ref[pl.ds(at, r)] = (keep_ref[i] + other_ref[i].astype(F32)).astype(BF16)


def core_sum(kept, given, tag, after=()):
    taken = lax.ppermute(given, WIDE, CORE_SWAP)
    groups, rows, depth = kept.shape
    b = rows // 4
    outs = [sds((groups, b, depth), F32)] + [sds((groups, b, depth), BF16)] * 3
    return simple_call(merge_kernel, [kept, taken], outs, [], 8e6, "merge_" + tag, after, WIDE_GRANT)


def x_exchange(blocks):
    return [lax.ppermute(block, WIDE, X_SHIFT[d]) for d, block in zip((1, 2, 3), blocks)]


def x_sum(own, got, tag, after=()):
    groups, b, depth = own.shape
    outs = [sds((groups, b // 2, depth), F32), sds((groups, b // 2, depth), BF16)]
    return simple_call(cross_kernel, [own, *got], outs, [], 2e6, "cross_" + tag, after, WIDE_GRANT)


def z_sum(place, keep, send, tag, after=()):
    other = lax.ppermute(send, WIDE, Z_SWAP)
    outs = [sds((keep.shape[0] * keep.shape[1], keep.shape[2]), BF16)]
    return simple_call(finish_kernel, [place, keep, other], outs, [], 1e6, "finish_" + tag, after, WIDE_GRANT)[0]


def wide_gather(rows, work):
    pair = jnp.stack([rows, lax.ppermute(rows, WIDE, Z_SWAP)])
    after = work(pair)
    blocks = [pair] + [lax.ppermute(pair, WIDE, X_SHIFT[(4 - d) % 4]) for d in (1, 2, 3)]
    mine = join(blocks, "join_rows")
    theirs = lax.ppermute(mine, WIDE, CORE_SWAP)
    shape = (mine.shape[0], 2, 4, mine.shape[1] // 8, mine.shape[2])
    return [mine.reshape(shape), theirs.reshape(shape)], after, mine


def update_kernel(s_ref, x0_ref, x1_ref, *refs):
    pieces, blocks_ref, out_ref, turned = refs[:5], refs[5], refs[6], refs[7]
    half, cols = pieces[4].shape
    depth = out_ref.shape[0]

    @pl.when(pl.program_id(0) == 0)
    def _():
        for i, g in enumerate((0, 1, 3, 2)):
            for core, ref in enumerate((x0_ref, x1_ref)):
                second = s_ref[1] if core == 0 else 1 - s_ref[1]
                at = pl.multiple_of((2 * i + second) * half, 128)
                turned[:, pl.ds(at, half)] = ref[:, g].reshape(half, depth).T

    rhs = jnp.concatenate([p[...] for p in pieces], axis=0)
    total = jnp.dot(turned[...], rhs, preferred_element_type=F32)
    out_ref[...] = (total + blocks_ref[...].reshape(depth, cols).astype(F32)).astype(BF16)


def update_call(place, x, k, pieces, gathered, name, after=()):
    half, width = pieces[4].shape
    blocks, _, groups, r, depth = x[0].shape
    parts, n_rows, _ = gathered.shape
    return call(
        update_kernel,
        place,
        (width // CB,),
        [(a, (blocks, None, groups, r, depth), lambda j, s: (0, k, 0, 0, 0)) for a in x]
        + [col(a) for a in pieces]
        + [(gathered, (parts, n_rows, CB), lambda j, s: (0, 0, j))],
        [col(sds((depth, width), BF16))],
        [pltpu.VMEM((depth, 8 * half), BF16)],
        62,
        (16 * half * depth * width, 16 * half * (depth + width) + 4 * depth * width),
        name,
        after,
    )[0]


def body(x_stash, token_ids, grad_out, w_up, w_down, acc_up, acc_down, offsets):
    narrow, wide = lax.axis_index(NARROW), lax.axis_index(WIDE)
    parts = lax.axis_size(WIDE)
    width = w_up.shape[1]
    where = jnp.stack([narrow // 2, narrow % 2, wide // 8]).astype(jnp.int32)
    base = (wide * x_stash.shape[0]).astype(jnp.int32)
    place = jnp.concatenate([where, offsets.reshape(2), base[None]])

    x, (to_up, to_down), joined = wide_gather(
        pick(place, token_ids, x_stash, grad_out),
        lambda pair: relay(place, acc_up, acc_down, width, parts, (pair,)),
    )
    half = half_rows(x)

    far, far_done = far_sum(place, x, w_up, w_down, ())
    down_blocks = exchange(hold(to_down, (joined,)))
    near_h, done = near_sum(place, x, 0, w_up, far, "hidden", (far_done,))
    near_b, done = near_sum(place, x, 1, w_down, far, "back", (done,))

    keep, other, done = own_sum(place, x, 0, w_up, near_h, "hidden", (done,))
    gelu_value, slope = gelu_parts(keep + other.astype(F32))
    mine = gelu_value.astype(BF16)
    act_other = lax.ppermute(mine, NARROW, ZHI_SWAP)
    keep, other, done = own_sum(place, x, 1, w_down, near_b, "back", (act_other, down_blocks))
    act, act_far = narrow_gather(mine, act_other, "act", (done,))
    hidden_grad = ((keep + other.astype(F32)) * slope).astype(BF16)
    grad_other = lax.ppermute(hidden_grad, NARROW, ZHI_SWAP)
    to_up = hold(to_up, (grad_other,))
    up_blocks = exchange(to_up)
    grad, _ = narrow_gather(hidden_grad, grad_other, "grad", (act_far[0], act_far[1], to_up), False)
    kept, given = rows_call(place, act + act_far, half, w_down, "out_rows", (grad[0],))
    near_done = (grad[1], grad[2])
    new_down = update_call(place, x, 1, act + act_far, down_blocks, "down_update", (given,))
    grad_far = far_gather(grad, (new_down, *near_done))
    own_out, *out_blocks = core_sum(kept, hold(given, near_done), "out")
    kept, given = rows_call(place, grad + grad_far, half, w_up, "grad_rows", (own_out,))
    out_got = x_exchange(out_blocks)
    own, *blocks = core_sum(kept, hold(given, (*out_got, up_blocks)), "grad")
    got = x_exchange(blocks)
    out_keep, out_send = x_sum(own_out, out_got, "out", (own,))
    new_up = update_call(place, x, 0, grad + grad_far, up_blocks, "up_update", (own, out_send))
    keep, send = x_sum(own, got, "grad", (new_up,))
    out_y = z_sum(place, out_keep, out_send, "out", (send,))
    grad_in = z_sum(place, keep, send, "grad", (out_y,))
    return (out_y, grad_in, new_up, new_down)


def solution(mesh):
    in_specs = (
        P("wide", "narrow"),
        P("wide"),
        P("wide", "narrow"),
        P("narrow", "wide"),
        P("narrow", "wide"),
        P("narrow", "wide", None),
        P("narrow", "wide", None),
        P(None, "narrow", "wide"),
    )
    out_specs = (P("wide", "narrow"), P("wide", "narrow"), P("narrow", "wide"), P("narrow", "wide"))
    return jax.shard_map(body, mesh=mesh, in_specs=in_specs, out_specs=out_specs, check_vma=False)
```

```python
import functools

import jax
import jax.numpy as jnp
from jax import lax
from jax.experimental import pallas as pl
from jax.experimental.pallas import tpu as pltpu
from jax.sharding import PartitionSpec as P

SLACK = 512
MIB = 2**20
SMALL = 16
WIDE_GRANT = 62
BF16 = jnp.bfloat16
F32 = jnp.float32
WIDE = "wide"
NARROW = "narrow"

CORE_SWAP = [(k, k ^ 1) for k in range(16)]
Z_SWAP = [(k, k ^ 8) for k in range(16)]
X_SHIFT = [[(k, (k & 8) | ((k + 2 * d) & 7)) for k in range(16)] for d in range(4)]
ZHI_SWAP = [(k, k ^ 1) for k in range(8)]
Y_RIGHT = [(k, (k + 2) % 8) for k in range(8)]
Y_LEFT = [(k, (k - 2) % 8) for k in range(8)]
CB = 384
DB = 256


def sds(shape, dtype):
    return jax.ShapeDtypeStruct(shape, dtype)


def cost(flops, nbytes):
    return pl.CostEstimate(flops=int(flops), bytes_accessed=int(nbytes), transcendentals=0)


def gelu_parts(hidden):
    normal_cdf = 0.5 * (1.0 + jax.scipy.special.erf(hidden * 0.7071067811865476))
    density = jnp.exp(-0.5 * hidden * hidden) * 0.3989422804014327
    return (hidden * normal_cdf, normal_cdf + hidden * density)


HBM = pl.BlockSpec(memory_space=pl.ANY)


def call(kernel, place, grid, ins, outs, scratch, mib, work, name, after=()):
    n, m = len(ins), len(after)

    def spec(block, index):
        return HBM if block is None else pl.BlockSpec(block, index)

    def run(s_ref, *refs):
        kernel(s_ref, *refs[:n], *refs[n + m :])

    return pl.pallas_call(
        run,
        out_shape=[shape for shape, _, _ in outs],
        grid_spec=pltpu.PrefetchScalarGridSpec(
            num_scalar_prefetch=1,
            grid=grid,
            in_specs=[spec(block, index) for _, block, index in ins] + [HBM] * m,
            out_specs=[pl.BlockSpec(block, index) for _, block, index in outs],
            scratch_shapes=scratch,
        ),
        compiler_params=pltpu.CompilerParams(vmem_limit_bytes=mib * MIB),
        cost_estimate=cost(*work),
        name=name,
    )(place, *[a for a, _, _ in ins], *after)


def whole(a):
    zeros = (0,) * a.ndim
    return (a, a.shape, lambda i, s: zeros)


def col(a):
    return (a, (a.shape[0], CB), lambda j, s: (0, j))


def pick_kernel(s_ref, ids_ref, stash_ref, grad_ref, out_ref, wide, rows):
    tokens = grad_ref.shape[0]
    n = tokens // 4
    wide[...] = stash_ref[...].astype(F32)
    for d in range(4):
        group = (s_ref[0] + d) % 4
        at = tokens + d * n
        out_ref[at : at + n] = grad_ref[pl.ds(pl.multiple_of(group * n, n), n)]
        for i in range(n):
            row = ids_ref[group * n + i] - s_ref[5]
            rows[d * n + i : d * n + i + 1] = wide[pl.ds(row, 1)]
    out_ref[:tokens] = rows[...].astype(BF16)


def simple_call(kernel, ins, outs, scratch, nbytes, name, after=(), mib=SMALL):
    n, m = len(ins), len(after)

    def run(*refs):
        kernel(*refs[:n], *refs[n + m :])

    def spec(a):
        return pl.BlockSpec(memory_space=pltpu.SMEM if a.dtype == jnp.int32 else pltpu.VMEM)

    return pl.pallas_call(
        run,
        out_shape=outs,
        in_specs=[spec(a) for a in ins] + [HBM] * m,
        out_specs=[pl.BlockSpec(memory_space=pltpu.VMEM)] * len(outs),
        scratch_shapes=scratch,
        compiler_params=pltpu.CompilerParams(vmem_limit_bytes=mib * MIB),
        cost_estimate=cost(0, nbytes),
        name=name,
    )(*ins, *after)


def pick(place, ids, stash, grad):
    return simple_call(
        pick_kernel,
        [place, ids, stash, grad],
        [sds((2 * grad.shape[0], grad.shape[1]), BF16)],
        [pltpu.VMEM(stash.shape, F32), pltpu.VMEM(grad.shape, F32)],
        2e6,
        "pick",
    )[0]


def hold(x, after):
    return pl.pallas_call(
        lambda *refs: None,
        out_shape=sds(x.shape, x.dtype),
        in_specs=[HBM] * (1 + len(after)),
        out_specs=HBM,
        input_output_aliases={0: 0},
        cost_estimate=cost(0, 0),
        name="hold",
    )(x, *after)


def join_kernel(*refs):
    at = 0
    for ref in refs[:-1]:
        refs[-1][at : at + ref.shape[0]] = ref[...]
        at += ref.shape[0]


def join(blocks, name, after=()):
    rows = sum(b.shape[0] for b in blocks)
    return simple_call(join_kernel, blocks, [sds((rows, *blocks[0].shape[1:]), BF16)], [], 2e6, name, after)[0]


STEP = 16


def relay_kernel(s_ref, up_ref, down_ref, to_up_ref, to_down_ref, seg, rows, sem):
    parts, _, width = rows.shape
    line = parts * width
    chunks = to_up_ref.shape[1] // STEP
    for i, ref in enumerate((up_ref, down_ref)):
        for c in range(chunks):
            at = pl.multiple_of(s_ref[3 + i] + c * STEP * line, 128)
            k = i * chunks + c
            pltpu.make_async_copy(ref.at[:, :, pl.ds(at, STEP * line)], seg.at[k], sem.at[k]).start()
    for i, ref in enumerate((up_ref, down_ref)):
        out_ref = (to_up_ref, to_down_ref)[i]
        for c in range(chunks):
            k = i * chunks + c
            pltpu.make_async_copy(ref.at[:, :, pl.ds(0, STEP * line)], seg.at[k], sem.at[k]).wait()

            @pl.loop(0, STEP)
            def _(r):
                for w in range(parts):
                    at = pl.multiple_of(r * line + w * width, 128)
                    rows[w, pl.ds(r, 1), :] = seg[k, 0, :, pl.ds(at, width)].astype(F32)

            @pl.loop(0, parts)
            def _(w):
                out_ref[w, c * STEP : (c + 1) * STEP] = rows[w].astype(BF16)


def relay(place, acc_up, acc_down, width, parts, after=()):
    line = width * parts
    n_rows = (acc_up.shape[2] - SLACK) // line
    n = len(after)

    def run(s_ref, up_ref, down_ref, *refs):
        relay_kernel(s_ref, up_ref, down_ref, *refs[n:])

    return pl.pallas_call(
        run,
        out_shape=[sds((parts, n_rows, width), BF16)] * 2,
        in_specs=[pl.BlockSpec(memory_space=pltpu.SMEM)] + [HBM] * (2 + n),
        out_specs=[pl.BlockSpec(memory_space=pltpu.VMEM)] * 2,
        scratch_shapes=[
            pltpu.VMEM((2 * n_rows // STEP, 1, 1, STEP * line), BF16),
            pltpu.VMEM((parts, STEP, width), F32),
            pltpu.SemaphoreType.DMA((2 * n_rows // STEP,)),
        ],
        compiler_params=pltpu.CompilerParams(vmem_limit_bytes=32 * MIB),
        cost_estimate=cost(0, 32e6),
        name="relay",
    )(place, acc_up, acc_down, *after)


def rows_of(ref0, ref1):
    depth = ref0.shape[-1]
    return jnp.concatenate([ref0[...].reshape(-1, depth), ref1[...].reshape(-1, depth)], axis=0)


def far_kernel(s_ref, x0_ref, x1_ref, g0_ref, g1_ref, up_ref, down_ref, a_ref, b_ref):
    half = a_ref.shape[1]
    for i, (r0, r1, w_ref) in enumerate(((x0_ref, x1_ref, up_ref), (g0_ref, g1_ref, down_ref))):
        total = jnp.dot(rows_of(r0, r1), w_ref[...], preferred_element_type=F32)
        a_ref[i] = total[:half].astype(BF16)
        b_ref[i] = total[half:].astype(BF16)


def near_kernel(s_ref, r0_ref, r1_ref, l0_ref, l1_ref, w_ref, a_ref, b_ref, right_ref, left_ref):
    half = a_ref.shape[1]
    right = jnp.dot(rows_of(r0_ref, r1_ref), w_ref[...], preferred_element_type=F32)
    right_ref[:half] = (right[:half] + a_ref[0].astype(F32)).astype(BF16)
    right_ref[half:] = right[half:].astype(BF16)
    left = jnp.dot(rows_of(l0_ref, l1_ref), w_ref[...], preferred_element_type=F32)
    left_ref[:half] = left[:half].astype(BF16)
    left_ref[half:] = (left[half:] + b_ref[0].astype(F32)).astype(BF16)


def own_kernel(s_ref, x0_ref, x1_ref, w_ref, p1_ref, p3_ref, keep_ref, send_ref):
    half = keep_ref.shape[0]
    total = jnp.dot(rows_of(x0_ref, x1_ref), w_ref[...], preferred_element_type=F32)
    total = total + p1_ref[...].astype(F32) + p3_ref[...].astype(F32)
    first = s_ref[1] == 0
    keep_ref[...] = jnp.where(first, total[:half], total[half:])
    send_ref[...] = jnp.where(first, total[half:], total[:half]).astype(BF16)


def rows_spec(a, i, k):
    blocks, _, _, r, depth = a.shape
    return (a, (blocks, None, 1, r, depth), lambda j, s: (0, i, k, 0, 0))


def layer(a, i):
    return (a, (1, a.shape[1], CB), lambda j, s: (i, 0, j))


def half_rows(x):
    return x[0].shape[0] * x[0].shape[3]


def feature_call(kernel, place, rows, ws, extra, outs, name, after=()):
    depth, width = ws[0].shape
    m = 128 * len(rows)
    return call(
        kernel,
        place,
        (width // CB,),
        rows + [col(w) for w in ws] + extra,
        outs,
        [],
        20,
        (2 * m * depth * width, 2 * depth * width + 2 * m * width),
        name,
        after,
    )


def far_sum(place, x, w_up, w_down, after=()):
    width = w_up.shape[1]
    out = layer(sds((2, half_rows(x), width), BF16), 0)
    out = (out[0], (2, half_rows(x), CB), lambda j, s: (0, 0, j))
    rows = [rows_spec(a, i, 2) for i in range(2) for a in x]
    a, b = feature_call(far_kernel, place, rows, (w_up, w_down), [], [out, out], "far", after)
    return (lax.ppermute(a, NARROW, Y_RIGHT), lax.ppermute(b, NARROW, Y_LEFT)), a


def near_sum(place, x, i, w, terms, tag, after=()):
    out = col(sds((2 * half_rows(x), w.shape[1]), BF16))
    rows = [rows_spec(a, i, k) for k in (1, 3) for a in x]
    extra = [layer(t, i) for t in terms]
    right, left = feature_call(near_kernel, place, rows, (w,), extra, [out, out], tag + "_near", after)
    return (lax.ppermute(right, NARROW, Y_RIGHT), lax.ppermute(left, NARROW, Y_LEFT)), right


def own_sum(place, x, i, w, terms, tag, after=()):
    outs = [col(sds((half_rows(x), w.shape[1]), dtype)) for dtype in (F32, BF16)]
    rows = [rows_spec(a, i, 0) for a in x]
    keep, send = feature_call(own_kernel, place, rows, (w,), [col(t) for t in terms], outs, tag + "_own", after)
    return keep, lax.ppermute(send, NARROW, ZHI_SWAP), send


def far_gather(pieces, after):
    _, nxt, prev = pieces
    half = nxt.shape[0] // 2
    near = prev[:half], nxt[half:]
    if after:
        near = [hold(a, after) for a in near]
    return [lax.ppermute(near[0], NARROW, Y_RIGHT), lax.ppermute(near[1], NARROW, Y_LEFT)]


def narrow_gather(mine, other, tag, after, far=True):
    own = join([mine, other], "join_" + tag, after)
    prev, nxt = lax.ppermute(own, NARROW, Y_RIGHT), lax.ppermute(own, NARROW, Y_LEFT)
    pieces = [own, nxt, prev]
    return pieces, far_gather(pieces, ()) if far else None


def exchange(blocks):
    return lax.all_to_all(blocks, WIDE, 0, 0, tiled=True)


def rows_kernel(s_ref, *refs):
    pieces, (w_ref, out0_ref, out1_ref, held, sem) = refs[:-5], refs[-5:]
    _, _, half, width = held.shape

    @pl.when(pl.program_id(0) == 0)
    def _():
        copies = []
        for ref in pieces:
            for i in range(ref.shape[0] // half):
                at = len(copies)
                second = s_ref[1] if at % 2 == 0 else 1 - s_ref[1]
                copy = pltpu.make_async_copy(ref.at[pl.ds(i * half, half)], held.at[at // 2, second], sem.at[at])
                copy.start()
                copies.append(copy)
        for copy in copies:
            copy.wait()

    total = lax.dot_general(
        held[...].reshape(-1, width), w_ref[...], (((1,), (1,)), ((), ())), preferred_element_type=F32
    )
    for g in range(held.shape[0]):
        at = g * 2 * half
        out0_ref[g] = total[at : at + half]
        out1_ref[g] = total[at + half : at + 2 * half]


def rows_call(place, pieces, half, w, name, after=()):
    width = pieces[0].shape[1]
    depth = w.shape[0]
    groups = sum(a.shape[0] for a in pieces) // (2 * half)

    def out():
        return (sds((groups, half, depth), F32), (groups, half, DB), lambda j, s: (0, 0, j))

    return call(
        rows_kernel,
        place,
        (depth // DB,),
        [(a, None, None) for a in pieces] + [(w, (DB, width), lambda j, s: (j, 0))],
        [out(), out()],
        [pltpu.VMEM((groups, 2, half, width), BF16), pltpu.SemaphoreType.DMA((2 * groups,))],
        62,
        (4 * groups * half * depth * width, 2 * depth * width + 4 * groups * half * (width + 4 * depth)),
        name,
        after,
    )


def merge_kernel(*refs):
    own_ref, outs = refs[-4], refs[-3:]
    n = (len(refs) - 4) // 2
    b = own_ref.shape[1]
    at = 0
    for i in range(n):
        for g in range(refs[i].shape[0]):
            own_ref[at] = refs[i][g, :b] + refs[n + i][g, :b]
            for d in range(1, 4):
                rows = slice(d * b, (d + 1) * b)
                outs[d - 1][at] = (refs[i][g, rows] + refs[n + i][g, rows]).astype(BF16)
            at += 1


def cross_kernel(own_ref, *refs):
    keep_ref, send_ref = refs[-2:]
    r = keep_ref.shape[1]
    for g in range(own_ref.shape[0]):
        total = own_ref[g] + refs[0][g].astype(F32) + refs[1][g].astype(F32) + refs[2][g].astype(F32)
        keep_ref[g] = total[:r]
        send_ref[g] = total[r:].astype(BF16)


def finish_kernel(s_ref, keep_ref, other_ref, out_ref):
    r = keep_ref.shape[1]
    for i, d in enumerate((0, 1, 3, 2)):
        at = pl.multiple_of(((s_ref[0] + d) % 4) * r, r)
        out_ref[pl.ds(at, r)] = (keep_ref[i] + other_ref[i].astype(F32)).astype(BF16)


def core_sum(kept, given, tag, after=()):
    taken = lax.ppermute(given, WIDE, CORE_SWAP)
    groups, rows, depth = kept.shape
    b = rows // 4
    outs = [sds((groups, b, depth), F32)] + [sds((groups, b, depth), BF16)] * 3
    return simple_call(merge_kernel, [kept, taken], outs, [], 8e6, "merge_" + tag, after, WIDE_GRANT)


def x_exchange(blocks):
    return [lax.ppermute(block, WIDE, X_SHIFT[d]) for d, block in zip((1, 2, 3), blocks)]


def x_sum(own, got, tag, after=()):
    groups, b, depth = own.shape
    outs = [sds((groups, b // 2, depth), F32), sds((groups, b // 2, depth), BF16)]
    return simple_call(cross_kernel, [own, *got], outs, [], 2e6, "cross_" + tag, after, WIDE_GRANT)


def z_sum(place, keep, send, tag, after=()):
    other = lax.ppermute(send, WIDE, Z_SWAP)
    outs = [sds((keep.shape[0] * keep.shape[1], keep.shape[2]), BF16)]
    return simple_call(finish_kernel, [place, keep, other], outs, [], 1e6, "finish_" + tag, after, WIDE_GRANT)[0]


def wide_gather(rows, work):
    pair = jnp.stack([rows, lax.ppermute(rows, WIDE, Z_SWAP)])
    after = work(pair)
    blocks = [pair] + [lax.ppermute(pair, WIDE, X_SHIFT[(4 - d) % 4]) for d in (1, 2, 3)]
    mine = join(blocks, "join_rows")
    theirs = lax.ppermute(mine, WIDE, CORE_SWAP)
    shape = (mine.shape[0], 2, 4, mine.shape[1] // 8, mine.shape[2])
    return [mine.reshape(shape), theirs.reshape(shape)], after, mine


def update_kernel(s_ref, x0_ref, x1_ref, *refs):
    pieces, blocks_ref, out_ref, turned = refs[:5], refs[5], refs[6], refs[7]
    half, cols = pieces[4].shape
    depth = out_ref.shape[0]

    @pl.when(pl.program_id(0) == 0)
    def _():
        for i, g in enumerate((0, 1, 3, 2)):
            for core, ref in enumerate((x0_ref, x1_ref)):
                second = s_ref[1] if core == 0 else 1 - s_ref[1]
                at = pl.multiple_of((2 * i + second) * half, 128)
                turned[:, pl.ds(at, half)] = ref[:, g].reshape(half, depth).T

    rhs = jnp.concatenate([p[...] for p in pieces], axis=0)
    total = jnp.dot(turned[...], rhs, preferred_element_type=F32)
    out_ref[...] = (total + blocks_ref[...].reshape(depth, cols).astype(F32)).astype(BF16)


def update_call(place, x, k, pieces, gathered, name, after=()):
    half, width = pieces[4].shape
    blocks, _, groups, r, depth = x[0].shape
    parts, n_rows, _ = gathered.shape
    return call(
        update_kernel,
        place,
        (width // CB,),
        [(a, (blocks, None, groups, r, depth), lambda j, s: (0, k, 0, 0, 0)) for a in x]
        + [col(a) for a in pieces]
        + [(gathered, (parts, n_rows, CB), lambda j, s: (0, 0, j))],
        [col(sds((depth, width), BF16))],
        [pltpu.VMEM((depth, 8 * half), BF16)],
        62,
        (16 * half * depth * width, 16 * half * (depth + width) + 4 * depth * width),
        name,
        after,
    )[0]


def body(x_stash, token_ids, grad_out, w_up, w_down, acc_up, acc_down, offsets):
    narrow, wide = lax.axis_index(NARROW), lax.axis_index(WIDE)
    parts = lax.axis_size(WIDE)
    width = w_up.shape[1]
    where = jnp.stack([narrow // 2, narrow % 2, wide // 8]).astype(jnp.int32)
    base = (wide * x_stash.shape[0]).astype(jnp.int32)
    place = jnp.concatenate([where, offsets.reshape(2), base[None]])

    x, (to_up, to_down), joined = wide_gather(
        pick(place, token_ids, x_stash, grad_out),
        lambda pair: relay(place, acc_up, acc_down, width, parts, (pair,)),
    )
    half = half_rows(x)

    far, far_done = far_sum(place, x, w_up, w_down, ())
    down_blocks = exchange(hold(to_down, (joined,)))
    near_h, done = near_sum(place, x, 0, w_up, far, "hidden", (far_done,))
    near_b, done = near_sum(place, x, 1, w_down, far, "back", (done,))

    keep, other, done = own_sum(place, x, 0, w_up, near_h, "hidden", (done,))
    gelu_value, slope = gelu_parts(keep + other.astype(F32))
    mine = gelu_value.astype(BF16)
    act_other = lax.ppermute(mine, NARROW, ZHI_SWAP)
    keep, other, done = own_sum(place, x, 1, w_down, near_b, "back", (act_other, down_blocks))
    act, act_far = narrow_gather(mine, act_other, "act", (done,))
    hidden_grad = ((keep + other.astype(F32)) * slope).astype(BF16)
    grad_other = lax.ppermute(hidden_grad, NARROW, ZHI_SWAP)
    to_up = hold(to_up, (grad_other,))
    up_blocks = exchange(to_up)
    grad, _ = narrow_gather(hidden_grad, grad_other, "grad", (act_far[0], act_far[1], to_up), False)
    kept, given = rows_call(place, act + act_far, half, w_down, "out_rows", (grad[0],))
    near_done = (grad[1], grad[2])
    new_down = update_call(place, x, 1, act + act_far, down_blocks, "down_update", (given,))
    grad_far = far_gather(grad, (new_down, *near_done))
    own_out, *out_blocks = core_sum(kept, hold(given, near_done), "out")
    kept, given = rows_call(place, grad + grad_far, half, w_up, "grad_rows", (own_out,))
    out_got = x_exchange(out_blocks)
    own, *blocks = core_sum(kept, hold(given, (*out_got, up_blocks)), "grad")
    got = x_exchange(blocks)
    out_keep, out_send = x_sum(own_out, out_got, "out", (own,))
    new_up = update_call(place, x, 0, grad + grad_far, up_blocks, "up_update", (own, out_send))
    keep, send = x_sum(own, got, "grad", (new_up,))
    out_y = z_sum(place, out_keep, out_send, "out", (send,))
    grad_in = z_sum(place, keep, send, "grad", (out_y,))
    return (out_y, grad_in, new_up, new_down)


def solution(mesh):
    in_specs = (
        P("wide", "narrow"),
        P("wide"),
        P("wide", "narrow"),
        P("narrow", "wide"),
        P("narrow", "wide"),
        P("narrow", "wide", None),
        P("narrow", "wide", None),
        P(None, "narrow", "wide"),
    )
    out_specs = (P("wide", "narrow"), P("wide", "narrow"), P("narrow", "wide"), P("narrow", "wide"))
    return jax.shard_map(body, mesh=mesh, in_specs=in_specs, out_specs=out_specs, check_vma=False)
```

```python
import functools

import jax
import jax.numpy as jnp
from jax import lax
from jax.experimental import pallas as pl
from jax.experimental.pallas import tpu as pltpu
from jax.sharding import PartitionSpec as P

SLACK = 512
MIB = 2**20
SMALL = 16
WIDE_GRANT = 62
BF16 = jnp.bfloat16
F32 = jnp.float32
WIDE = "wide"
NARROW = "narrow"

CORE_SWAP = [(k, k ^ 1) for k in range(16)]
Z_SWAP = [(k, k ^ 8) for k in range(16)]
X_SHIFT = [[(k, (k & 8) | ((k + 2 * d) & 7)) for k in range(16)] for d in range(4)]
ZHI_SWAP = [(k, k ^ 1) for k in range(8)]
Y_RIGHT = [(k, (k + 2) % 8) for k in range(8)]
Y_LEFT = [(k, (k - 2) % 8) for k in range(8)]
CB = 640
DB = 256


def sds(shape, dtype):
    return jax.ShapeDtypeStruct(shape, dtype)


def cost(flops, nbytes):
    return pl.CostEstimate(flops=int(flops), bytes_accessed=int(nbytes), transcendentals=0)


def gelu_parts(hidden):
    normal_cdf = 0.5 * (1.0 + jax.scipy.special.erf(hidden * 0.7071067811865476))
    density = jnp.exp(-0.5 * hidden * hidden) * 0.3989422804014327
    return (hidden * normal_cdf, normal_cdf + hidden * density)


HBM = pl.BlockSpec(memory_space=pl.ANY)


def call(kernel, place, grid, ins, outs, scratch, mib, work, name, after=()):
    n, m = len(ins), len(after)

    def spec(block, index):
        return HBM if block is None else pl.BlockSpec(block, index)

    def run(s_ref, *refs):
        kernel(s_ref, *refs[:n], *refs[n + m :])

    return pl.pallas_call(
        run,
        out_shape=[shape for shape, _, _ in outs],
        grid_spec=pltpu.PrefetchScalarGridSpec(
            num_scalar_prefetch=1,
            grid=grid,
            in_specs=[spec(block, index) for _, block, index in ins] + [HBM] * m,
            out_specs=[pl.BlockSpec(block, index) for _, block, index in outs],
            scratch_shapes=scratch,
        ),
        compiler_params=pltpu.CompilerParams(vmem_limit_bytes=mib * MIB),
        cost_estimate=cost(*work),
        name=name,
    )(place, *[a for a, _, _ in ins], *after)


def whole(a):
    zeros = (0,) * a.ndim
    return (a, a.shape, lambda i, s: zeros)


def col(a):
    return (a, (a.shape[0], CB), lambda j, s: (0, j))


def pick_kernel(s_ref, ids_ref, stash_ref, grad_ref, out_ref, wide, rows):
    tokens = grad_ref.shape[0]
    n = tokens // 4
    wide[...] = stash_ref[...].astype(F32)
    for d in range(4):
        group = (s_ref[0] + d) % 4
        at = tokens + d * n
        out_ref[at : at + n] = grad_ref[pl.ds(pl.multiple_of(group * n, n), n)]
        for i in range(n):
            row = ids_ref[group * n + i] - s_ref[5]
            rows[d * n + i : d * n + i + 1] = wide[pl.ds(row, 1)]
    out_ref[:tokens] = rows[...].astype(BF16)


def simple_call(kernel, ins, outs, scratch, nbytes, name, after=(), mib=SMALL):
    n, m = len(ins), len(after)

    def run(*refs):
        kernel(*refs[:n], *refs[n + m :])

    def spec(a):
        return pl.BlockSpec(memory_space=pltpu.SMEM if a.dtype == jnp.int32 else pltpu.VMEM)

    return pl.pallas_call(
        run,
        out_shape=outs,
        in_specs=[spec(a) for a in ins] + [HBM] * m,
        out_specs=[pl.BlockSpec(memory_space=pltpu.VMEM)] * len(outs),
        scratch_shapes=scratch,
        compiler_params=pltpu.CompilerParams(vmem_limit_bytes=mib * MIB),
        cost_estimate=cost(0, nbytes),
        name=name,
    )(*ins, *after)


def pick(place, ids, stash, grad):
    return simple_call(
        pick_kernel,
        [place, ids, stash, grad],
        [sds((2 * grad.shape[0], grad.shape[1]), BF16)],
        [pltpu.VMEM(stash.shape, F32), pltpu.VMEM(grad.shape, F32)],
        2e6,
        "pick",
    )[0]


def hold(x, after):
    return pl.pallas_call(
        lambda *refs: None,
        out_shape=sds(x.shape, x.dtype),
        in_specs=[HBM] * (1 + len(after)),
        out_specs=HBM,
        input_output_aliases={0: 0},
        cost_estimate=cost(0, 0),
        name="hold",
    )(x, *after)


def join_kernel(*refs):
    at = 0
    for ref in refs[:-1]:
        refs[-1][at : at + ref.shape[0]] = ref[...]
        at += ref.shape[0]


def join(blocks, name, after=()):
    rows = sum(b.shape[0] for b in blocks)
    return simple_call(join_kernel, blocks, [sds((rows, *blocks[0].shape[1:]), BF16)], [], 2e6, name, after)[0]


STEP = 16


def relay_kernel(s_ref, up_ref, down_ref, to_up_ref, to_down_ref, seg, rows, sem):
    parts, _, width = rows.shape
    line = parts * width
    chunks = to_up_ref.shape[1] // STEP
    for i, ref in enumerate((up_ref, down_ref)):
        for c in range(chunks):
            at = pl.multiple_of(s_ref[3 + i] + c * STEP * line, 128)
            k = i * chunks + c
            pltpu.make_async_copy(ref.at[:, :, pl.ds(at, STEP * line)], seg.at[k], sem.at[k]).start()
    for i, ref in enumerate((up_ref, down_ref)):
        out_ref = (to_up_ref, to_down_ref)[i]
        for c in range(chunks):
            k = i * chunks + c
            pltpu.make_async_copy(ref.at[:, :, pl.ds(0, STEP * line)], seg.at[k], sem.at[k]).wait()

            @pl.loop(0, STEP)
            def _(r):
                for w in range(parts):
                    at = pl.multiple_of(r * line + w * width, 128)
                    rows[w, pl.ds(r, 1), :] = seg[k, 0, :, pl.ds(at, width)].astype(F32)

            @pl.loop(0, parts)
            def _(w):
                out_ref[w, c * STEP : (c + 1) * STEP] = rows[w].astype(BF16)


def relay(place, acc_up, acc_down, width, parts, after=()):
    line = width * parts
    n_rows = (acc_up.shape[2] - SLACK) // line
    n = len(after)

    def run(s_ref, up_ref, down_ref, *refs):
        relay_kernel(s_ref, up_ref, down_ref, *refs[n:])

    return pl.pallas_call(
        run,
        out_shape=[sds((parts, n_rows, width), BF16)] * 2,
        in_specs=[pl.BlockSpec(memory_space=pltpu.SMEM)] + [HBM] * (2 + n),
        out_specs=[pl.BlockSpec(memory_space=pltpu.VMEM)] * 2,
        scratch_shapes=[
            pltpu.VMEM((2 * n_rows // STEP, 1, 1, STEP * line), BF16),
            pltpu.VMEM((parts, STEP, width), F32),
            pltpu.SemaphoreType.DMA((2 * n_rows // STEP,)),
        ],
        compiler_params=pltpu.CompilerParams(vmem_limit_bytes=32 * MIB),
        cost_estimate=cost(0, 32e6),
        name="relay",
    )(place, acc_up, acc_down, *after)


def rows_of(ref0, ref1):
    depth = ref0.shape[-1]
    return jnp.concatenate([ref0[...].reshape(-1, depth), ref1[...].reshape(-1, depth)], axis=0)


def far_kernel(s_ref, x0_ref, x1_ref, g0_ref, g1_ref, up_ref, down_ref, a_ref, b_ref):
    half = a_ref.shape[1]
    for i, (r0, r1, w_ref) in enumerate(((x0_ref, x1_ref, up_ref), (g0_ref, g1_ref, down_ref))):
        total = jnp.dot(rows_of(r0, r1), w_ref[...], preferred_element_type=F32)
        a_ref[i] = total[:half].astype(BF16)
        b_ref[i] = total[half:].astype(BF16)


def near_kernel(s_ref, r0_ref, r1_ref, l0_ref, l1_ref, w_ref, a_ref, b_ref, right_ref, left_ref):
    half = a_ref.shape[1]
    right = jnp.dot(rows_of(r0_ref, r1_ref), w_ref[...], preferred_element_type=F32)
    right_ref[:half] = (right[:half] + a_ref[0].astype(F32)).astype(BF16)
    right_ref[half:] = right[half:].astype(BF16)
    left = jnp.dot(rows_of(l0_ref, l1_ref), w_ref[...], preferred_element_type=F32)
    left_ref[:half] = left[:half].astype(BF16)
    left_ref[half:] = (left[half:] + b_ref[0].astype(F32)).astype(BF16)


def own_kernel(s_ref, x0_ref, x1_ref, w_ref, p1_ref, p3_ref, keep_ref, send_ref):
    half = keep_ref.shape[0]
    total = jnp.dot(rows_of(x0_ref, x1_ref), w_ref[...], preferred_element_type=F32)
    total = total + p1_ref[...].astype(F32) + p3_ref[...].astype(F32)
    first = s_ref[1] == 0
    keep_ref[...] = jnp.where(first, total[:half], total[half:])
    send_ref[...] = jnp.where(first, total[half:], total[:half]).astype(BF16)


def rows_spec(a, i, k):
    blocks, _, _, r, depth = a.shape
    return (a, (blocks, None, 1, r, depth), lambda j, s: (0, i, k, 0, 0))


def layer(a, i):
    return (a, (1, a.shape[1], CB), lambda j, s: (i, 0, j))


def half_rows(x):
    return x[0].shape[0] * x[0].shape[3]


def feature_call(kernel, place, rows, ws, extra, outs, name, after=()):
    depth, width = ws[0].shape
    m = 128 * len(rows)
    return call(
        kernel,
        place,
        (width // CB,),
        rows + [col(w) for w in ws] + extra,
        outs,
        [],
        20,
        (2 * m * depth * width, 2 * depth * width + 2 * m * width),
        name,
        after,
    )


def far_sum(place, x, w_up, w_down, after=()):
    width = w_up.shape[1]
    out = layer(sds((2, half_rows(x), width), BF16), 0)
    out = (out[0], (2, half_rows(x), CB), lambda j, s: (0, 0, j))
    rows = [rows_spec(a, i, 2) for i in range(2) for a in x]
    a, b = feature_call(far_kernel, place, rows, (w_up, w_down), [], [out, out], "far", after)
    return (lax.ppermute(a, NARROW, Y_RIGHT), lax.ppermute(b, NARROW, Y_LEFT)), a


def near_sum(place, x, i, w, terms, tag, after=()):
    out = col(sds((2 * half_rows(x), w.shape[1]), BF16))
    rows = [rows_spec(a, i, k) for k in (1, 3) for a in x]
    extra = [layer(t, i) for t in terms]
    right, left = feature_call(near_kernel, place, rows, (w,), extra, [out, out], tag + "_near", after)
    return (lax.ppermute(right, NARROW, Y_RIGHT), lax.ppermute(left, NARROW, Y_LEFT)), right


def own_sum(place, x, i, w, terms, tag, after=()):
    outs = [col(sds((half_rows(x), w.shape[1]), dtype)) for dtype in (F32, BF16)]
    rows = [rows_spec(a, i, 0) for a in x]
    keep, send = feature_call(own_kernel, place, rows, (w,), [col(t) for t in terms], outs, tag + "_own", after)
    return keep, lax.ppermute(send, NARROW, ZHI_SWAP), send


def far_gather(pieces, after):
    _, nxt, prev = pieces
    half = nxt.shape[0] // 2
    near = prev[:half], nxt[half:]
    if after:
        near = [hold(a, after) for a in near]
    return [lax.ppermute(near[0], NARROW, Y_RIGHT), lax.ppermute(near[1], NARROW, Y_LEFT)]


def narrow_gather(mine, other, tag, after, far=True):
    own = join([mine, other], "join_" + tag, after)
    prev, nxt = lax.ppermute(own, NARROW, Y_RIGHT), lax.ppermute(own, NARROW, Y_LEFT)
    pieces = [own, nxt, prev]
    return pieces, far_gather(pieces, ()) if far else None


def exchange(blocks):
    return lax.all_to_all(blocks, WIDE, 0, 0, tiled=True)


def rows_kernel(s_ref, *refs):
    pieces, (w_ref, out0_ref, out1_ref, held, sem) = refs[:-5], refs[-5:]
    _, _, half, width = held.shape

    @pl.when(pl.program_id(0) == 0)
    def _():
        copies = []
        for ref in pieces:
            for i in range(ref.shape[0] // half):
                at = len(copies)
                second = s_ref[1] if at % 2 == 0 else 1 - s_ref[1]
                copy = pltpu.make_async_copy(ref.at[pl.ds(i * half, half)], held.at[at // 2, second], sem.at[at])
                copy.start()
                copies.append(copy)
        for copy in copies:
            copy.wait()

    total = lax.dot_general(
        held[...].reshape(-1, width), w_ref[...], (((1,), (1,)), ((), ())), preferred_element_type=F32
    )
    for g in range(held.shape[0]):
        at = g * 2 * half
        out0_ref[g] = total[at : at + half]
        out1_ref[g] = total[at + half : at + 2 * half]


def rows_call(place, pieces, half, w, name, after=()):
    width = pieces[0].shape[1]
    depth = w.shape[0]
    groups = sum(a.shape[0] for a in pieces) // (2 * half)

    def out():
        return (sds((groups, half, depth), F32), (groups, half, DB), lambda j, s: (0, 0, j))

    return call(
        rows_kernel,
        place,
        (depth // DB,),
        [(a, None, None) for a in pieces] + [(w, (DB, width), lambda j, s: (j, 0))],
        [out(), out()],
        [pltpu.VMEM((groups, 2, half, width), BF16), pltpu.SemaphoreType.DMA((2 * groups,))],
        62,
        (4 * groups * half * depth * width, 2 * depth * width + 4 * groups * half * (width + 4 * depth)),
        name,
        after,
    )


def merge_kernel(*refs):
    own_ref, outs = refs[-4], refs[-3:]
    n = (len(refs) - 4) // 2
    b = own_ref.shape[1]
    at = 0
    for i in range(n):
        for g in range(refs[i].shape[0]):
            own_ref[at] = refs[i][g, :b] + refs[n + i][g, :b]
            for d in range(1, 4):
                rows = slice(d * b, (d + 1) * b)
                outs[d - 1][at] = (refs[i][g, rows] + refs[n + i][g, rows]).astype(BF16)
            at += 1


def cross_kernel(own_ref, *refs):
    keep_ref, send_ref = refs[-2:]
    r = keep_ref.shape[1]
    for g in range(own_ref.shape[0]):
        total = own_ref[g] + refs[0][g].astype(F32) + refs[1][g].astype(F32) + refs[2][g].astype(F32)
        keep_ref[g] = total[:r]
        send_ref[g] = total[r:].astype(BF16)


def finish_kernel(s_ref, keep_ref, other_ref, out_ref):
    r = keep_ref.shape[1]
    for i, d in enumerate((0, 1, 3, 2)):
        at = pl.multiple_of(((s_ref[0] + d) % 4) * r, r)
        out_ref[pl.ds(at, r)] = (keep_ref[i] + other_ref[i].astype(F32)).astype(BF16)


def core_sum(kept, given, tag, after=()):
    taken = lax.ppermute(given, WIDE, CORE_SWAP)
    groups, rows, depth = kept.shape
    b = rows // 4
    outs = [sds((groups, b, depth), F32)] + [sds((groups, b, depth), BF16)] * 3
    return simple_call(merge_kernel, [kept, taken], outs, [], 8e6, "merge_" + tag, after, WIDE_GRANT)


def x_exchange(blocks):
    return [lax.ppermute(block, WIDE, X_SHIFT[d]) for d, block in zip((1, 2, 3), blocks)]


def x_sum(own, got, tag, after=()):
    groups, b, depth = own.shape
    outs = [sds((groups, b // 2, depth), F32), sds((groups, b // 2, depth), BF16)]
    return simple_call(cross_kernel, [own, *got], outs, [], 2e6, "cross_" + tag, after, WIDE_GRANT)


def z_sum(place, keep, send, tag, after=()):
    other = lax.ppermute(send, WIDE, Z_SWAP)
    outs = [sds((keep.shape[0] * keep.shape[1], keep.shape[2]), BF16)]
    return simple_call(finish_kernel, [place, keep, other], outs, [], 1e6, "finish_" + tag, after, WIDE_GRANT)[0]


def wide_gather(rows, work):
    pair = jnp.stack([rows, lax.ppermute(rows, WIDE, Z_SWAP)])
    after = work(pair)
    blocks = [pair] + [lax.ppermute(pair, WIDE, X_SHIFT[(4 - d) % 4]) for d in (1, 2, 3)]
    mine = join(blocks, "join_rows")
    theirs = lax.ppermute(mine, WIDE, CORE_SWAP)
    shape = (mine.shape[0], 2, 4, mine.shape[1] // 8, mine.shape[2])
    return [mine.reshape(shape), theirs.reshape(shape)], after, mine


def update_kernel(s_ref, x0_ref, x1_ref, *refs):
    pieces, blocks_ref, out_ref, turned = refs[:5], refs[5], refs[6], refs[7]
    half, cols = pieces[4].shape
    depth = out_ref.shape[0]

    @pl.when(pl.program_id(0) == 0)
    def _():
        for i, g in enumerate((0, 1, 3, 2)):
            for core, ref in enumerate((x0_ref, x1_ref)):
                second = s_ref[1] if core == 0 else 1 - s_ref[1]
                at = pl.multiple_of((2 * i + second) * half, 128)
                turned[:, pl.ds(at, half)] = ref[:, g].reshape(half, depth).T

    rhs = jnp.concatenate([p[...] for p in pieces], axis=0)
    total = jnp.dot(turned[...], rhs, preferred_element_type=F32)
    out_ref[...] = (total + blocks_ref[...].reshape(depth, cols).astype(F32)).astype(BF16)


def update_call(place, x, k, pieces, gathered, name, after=()):
    half, width = pieces[4].shape
    blocks, _, groups, r, depth = x[0].shape
    parts, n_rows, _ = gathered.shape
    return call(
        update_kernel,
        place,
        (width // CB,),
        [(a, (blocks, None, groups, r, depth), lambda j, s: (0, k, 0, 0, 0)) for a in x]
        + [col(a) for a in pieces]
        + [(gathered, (parts, n_rows, CB), lambda j, s: (0, 0, j))],
        [col(sds((depth, width), BF16))],
        [pltpu.VMEM((depth, 8 * half), BF16)],
        62,
        (16 * half * depth * width, 16 * half * (depth + width) + 4 * depth * width),
        name,
        after,
    )[0]


def body(x_stash, token_ids, grad_out, w_up, w_down, acc_up, acc_down, offsets):
    narrow, wide = lax.axis_index(NARROW), lax.axis_index(WIDE)
    parts = lax.axis_size(WIDE)
    width = w_up.shape[1]
    where = jnp.stack([narrow // 2, narrow % 2, wide // 8]).astype(jnp.int32)
    base = (wide * x_stash.shape[0]).astype(jnp.int32)
    place = jnp.concatenate([where, offsets.reshape(2), base[None]])

    x, (to_up, to_down), joined = wide_gather(
        pick(place, token_ids, x_stash, grad_out),
        lambda pair: relay(place, acc_up, acc_down, width, parts, (pair,)),
    )
    half = half_rows(x)

    far, far_done = far_sum(place, x, w_up, w_down, ())
    down_blocks = exchange(hold(to_down, (joined,)))
    near_h, done = near_sum(place, x, 0, w_up, far, "hidden", (far_done,))
    near_b, done = near_sum(place, x, 1, w_down, far, "back", (done,))

    keep, other, done = own_sum(place, x, 0, w_up, near_h, "hidden", (done,))
    gelu_value, slope = gelu_parts(keep + other.astype(F32))
    mine = gelu_value.astype(BF16)
    act_other = lax.ppermute(mine, NARROW, ZHI_SWAP)
    keep, other, done = own_sum(place, x, 1, w_down, near_b, "back", (act_other, down_blocks))
    act, act_far = narrow_gather(mine, act_other, "act", (done,))
    hidden_grad = ((keep + other.astype(F32)) * slope).astype(BF16)
    grad_other = lax.ppermute(hidden_grad, NARROW, ZHI_SWAP)
    to_up = hold(to_up, (grad_other,))
    up_blocks = exchange(to_up)
    grad, _ = narrow_gather(hidden_grad, grad_other, "grad", (act_far[0], act_far[1], to_up), False)
    kept, given = rows_call(place, act + act_far, half, w_down, "out_rows", (grad[0],))
    near_done = (grad[1], grad[2])
    new_down = update_call(place, x, 1, act + act_far, down_blocks, "down_update", (given,))
    grad_far = far_gather(grad, (new_down, *near_done))
    own_out, *out_blocks = core_sum(kept, hold(given, near_done), "out")
    kept, given = rows_call(place, grad + grad_far, half, w_up, "grad_rows", (own_out,))
    out_got = x_exchange(out_blocks)
    own, *blocks = core_sum(kept, hold(given, (*out_got, up_blocks)), "grad")
    got = x_exchange(blocks)
    out_keep, out_send = x_sum(own_out, out_got, "out", (own,))
    new_up = update_call(place, x, 0, grad + grad_far, up_blocks, "up_update", (own, out_send))
    keep, send = x_sum(own, got, "grad", (new_up,))
    out_y = z_sum(place, out_keep, out_send, "out", (send,))
    grad_in = z_sum(place, keep, send, "grad", (out_y,))
    return (out_y, grad_in, new_up, new_down)


def solution(mesh):
    in_specs = (
        P("wide", "narrow"),
        P("wide"),
        P("wide", "narrow"),
        P("narrow", "wide"),
        P("narrow", "wide"),
        P("narrow", "wide", None),
        P("narrow", "wide", None),
        P(None, "narrow", "wide"),
    )
    out_specs = (P("wide", "narrow"), P("wide", "narrow"), P("narrow", "wide"), P("narrow", "wide"))
    return jax.shard_map(body, mesh=mesh, in_specs=in_specs, out_specs=out_specs, check_vma=False)
```
